768 devices in a mesh: replica: 16 (over y, core), shard: 48 (over z, x).
Axes of the slice: x: 4, y: 8, z: 12, core: 2. Of those that a mesh axis runs over, the one named last changes fastest.
Arguments:
- table: bfloat16 [196608, 256], P('shard'), may hold values from -1.796875 to 1.796875
- row_state: float32 [196608], P('shard'), may hold values from 0.01 to 0.1
- touched_rows: int32 [49152], P('shard'), may hold values from 0 to 4095, as said below
- lookup_rows: int32 [16, 2304, 20], P('replica', 'shard'), may hold values from 0 to 4095, as said below
- lookup_bags: int32 [16, 2304, 20], P('replica', 'shard'), may hold values from 0 to 39
- route_counts: int32 [16, 2304], P('replica', 'shard'), may hold values from 5 to 20, as said below
- pooled_grad: float32 [30720, 256], P(('replica', 'shard')), may hold values from -6 to 6
Outputs:
- pooled: float32 [30720, 256], P(('replica', 'shard'))
- new_table: bfloat16 [196608, 256], P('shard')
- new_state: float32 [196608], P('shard')
The draws below stay inside these ranges and needn't reach their ends.
Inputs may be any that keep to these rules, and one draw needn't show every extreme that they name: `touched_rows`: each shard's 1024 entries are distinct, and every slot's row (live or not) is listed for its owning shard d. `lookup_rows`: every entry is listed in touched_rows for the owning shard d of its pair s * 48 + d. `route_counts`: in every draw one owning shard receives 20 live slots from every sender.
All inputs are finite; a program needn't handle non-finite values.
Results may differ from the reference program's by a relative error of at most 0.004.
Values may be sent and summed in bfloat16 or wider, within the bound.
No kernel may reach another device: no remote copies, remote signals or barrier semaphores. Data moves between devices by JAX's collectives and lax.ppermute only.
A program may use at most 32 MiB of HBM per device.

```python
import math
import jax
import jax.numpy as jnp
from jax import lax

E = 256
ROWS_DEV = 4096
TOUCH = 1024
BAGS_DEV = 40
CAP = 20
REPLICAS = 16
PAIRS = 2304
ROWS = 196608
BAGS = 30720
N_SHARD = 48


def touched_table(key):
    key_list = jax.random.split(key, N_SHARD)

    def one_order(sub_key):
        return jax.random.permutation(sub_key, ROWS_DEV)
    row_orders = jax.vmap(one_order)(key_list)
    return row_orders[:, :TOUCH].astype(jnp.int32)


def draw_touched_rows(key, part):
    shared = touched_table(key)
    return shared.reshape(-1).astype(jnp.int32)


def draw_lookup_rows(key, part):
    listed = touched_table(key)
    key = jax.random.fold_in(key, 2)
    positions = jax.random.randint(key, (REPLICAS, PAIRS, CAP), 0, TOUCH)
    dest_shard = jnp.arange(PAIRS, dtype=jnp.int32) % N_SHARD
    return listed[dest_shard[None, :, None], positions].astype(jnp.int32)


def draw_route_counts(key, part):
    key = jax.random.fold_in(key, 3)
    first_key, second_key = jax.random.split(key)
    counts = jax.random.randint(first_key, (REPLICAS, PAIRS), CAP // 4, CAP + 1)
    full_shard = jax.random.randint(second_key, (), 0, N_SHARD)
    dest_shard = jnp.arange(PAIRS, dtype=jnp.int32) % N_SHARD
    return jnp.where(dest_shard[None, :] == full_shard, CAP, counts).astype(jnp.int32)


def plant(drawn, own_key, smallest, top_value):
    index_at = [jax.random.randint(jax.random.fold_in(own_key, axis), (), 0, length) for axis, length in enumerate(drawn.shape)]
    main_axis = drawn.shape.index(max(drawn.shape))
    neighbour = index_at[:main_axis] + [(index_at[main_axis] + 1) % drawn.shape[main_axis]] + index_at[main_axis + 1:]
    return drawn.at[tuple(index_at)].set(smallest).at[tuple(neighbour)].set(top_value)


def level_of(key, dims, cuts, smallest, high):
    level = 1.0
    for axis_at, blocks in cuts:
        draws = jax.random.uniform(jax.random.fold_in(jax.random.fold_in(key, 6), axis_at), (blocks,), jnp.float32, smallest / len(cuts), high / len(cuts))
        level = level * jnp.repeat(jnp.exp(draws), dims[axis_at] // blocks).reshape((-1,) + (1,) * (len(dims) - 1 - axis_at))
    return level


def normal_values(rng, shape, scale, limit, cuts=(), held_as=jnp.bfloat16):
    entries = jax.random.normal(rng, shape, jnp.float32) * scale
    if len(cuts) > 0:
        entries = level_of(rng, shape, cuts, -0.22, 0.18) * entries
    return jnp.clip(entries, min=-limit, max=limit).astype(held_as)


def setup_inputs(seed: int = 0) -> dict:
    key_of = jax.random.split(jax.random.key(seed), 8)
    return {
        "table": normal_values(key_of[0], (ROWS, E), 0.3, 1.796875, ((0, 48),)),
        "row_state": jnp.clip(jnp.exp(math.log(0.1) - 2.3025851 * jax.random.uniform(key_of[1], (ROWS,), jnp.float32) ** level_of(key_of[1], (ROWS,), ((0, 48),), -0.2, 0.2)), 0.01, 0.1),
        "touched_rows": draw_touched_rows(jax.random.fold_in(key_of[7], 71), 0),
        "lookup_rows": draw_lookup_rows(jax.random.fold_in(key_of[7], 71), 0),
        "lookup_bags": plant(jax.random.randint(key_of[4], (REPLICAS, PAIRS, CAP), 0, BAGS_DEV), jax.random.fold_in(key_of[4], 1), 0, BAGS_DEV - 1).astype(jnp.int32),
        "route_counts": draw_route_counts(jax.random.fold_in(key_of[7], 71), 0),
        "pooled_grad": normal_values(key_of[6], (BAGS, E), 1.0, 6.0, ((0, 768),), jnp.float32),
    }


learn_rate = 0.5
epsilon = 1e-08

def reference(table, row_state, touched_rows, lookup_rows, lookup_bags, route_counts, pooled_grad):
    slot_ids = jnp.arange(CAP, dtype=jnp.int32)
    pair_ids = jnp.arange(PAIRS, dtype=jnp.int32)
    dest_shard = pair_ids % N_SHARD
    source = pair_ids // N_SHARD
    replica_ids = jnp.arange(REPLICAS, dtype=jnp.int32)

    def per_replica(totals, inputs):
        row_ids, bag_list, counts, replica_id = inputs
        live_mask = slot_ids[None, :] < counts[:, None]
        glob_rows = (dest_shard[:, None] * ROWS_DEV + row_ids).reshape(-1).astype(jnp.int32)
        glob_bags = ((replica_id * N_SHARD + source[:, None]) * BAGS_DEV + bag_list).reshape(-1).astype(jnp.int32)
        weight = live_mask.reshape(-1).astype(jnp.float32)[:, None]
        picked = jnp.take(table, glob_rows, axis=0).astype(jnp.float32) * weight
        pooled_part = jax.ops.segment_sum(picked, glob_bags, num_segments=BAGS)
        slot_grad = jnp.take(pooled_grad, glob_bags, axis=0) * weight
        row_part = jax.ops.segment_sum(slot_grad, glob_rows, num_segments=ROWS)
        return ((totals[0] + pooled_part, totals[1] + row_part), None)
    start = (jnp.zeros((BAGS, E), jnp.float32), jnp.zeros((ROWS, E), jnp.float32))
    (pooled, grad_sum), _ = lax.scan(per_replica, start, (lookup_rows, lookup_bags, route_counts, replica_ids))
    mean_grad = grad_sum / REPLICAS
    touched = (jnp.arange(N_SHARD * TOUCH, dtype=jnp.int32) // TOUCH * ROWS_DEV + touched_rows).astype(jnp.int32)
    grad_rows = jnp.take(mean_grad, touched, axis=0)
    state_now = jnp.take(row_state, touched) + lax.optimization_barrier(jnp.mean(grad_rows * grad_rows, axis=1))
    previous = jnp.take(table, touched, axis=0).astype(jnp.float32)
    updated = (previous - learn_rate * grad_rows / (jnp.sqrt(state_now)[:, None] + epsilon)).astype(jnp.bfloat16)
    return (pooled, table.at[touched].set(updated), row_state.at[touched].set(state_now))
```

```python
import functools

import jax
import jax.numpy as jnp
from jax import lax
from jax.experimental import pallas as pl
from jax.experimental.pallas import tpu as pltpu
from jax.sharding import PartitionSpec as P

learn_rate = 0.5
epsilon = 1e-08
bf16 = jnp.bfloat16
f32 = jnp.float32

block = 24
dead = 200
params = pltpu.CompilerParams(vmem_limit_bytes=24 * 1024 * 1024)


def iota(shape, axis):
    return lax.broadcasted_iota(jnp.int32, shape, axis)


def dot(a, b):
    return jnp.dot(a, b, preferred_element_type=f32)


def pair_of(position):
    return (position * 2731) >> 16


def slot_of(shape):
    position = iota(shape, 0)
    return position - block * pair_of(position)


def spread_matrix(shards):
    shape = (shards * block, shards)
    return jnp.where(pair_of(iota(shape, 0)) == iota(shape, 1), 1.0, 0.0)


def prep_kernel(rows_ref, bags_ref, counts_ref, grad_ref, out_ref, member_ref):
    shards, capacity = rows_ref.shape
    bag_count, width = grad_ref.shape
    flat = shards * block
    same = iota((shards, shards), 0) == iota((shards, shards), 1)
    counts = jnp.sum(
        jnp.where(same, counts_ref[...].astype(f32), 0.0), axis=1, keepdims=True
    )
    live = iota((shards, capacity), 1).astype(f32) < counts
    key = jnp.where(live, bags_ref[...], dead).astype(f32).astype(bf16)
    spread = spread_matrix(shards)
    spread_b = spread.astype(bf16)
    per_row = dot(spread_b, key)
    own = slot_of((flat, capacity)) == iota((flat, capacity), 1)
    bag = dot(jnp.where(own, per_row, 0.0).astype(bf16), jnp.ones((capacity, 128), bf16))
    match = (bag == iota((flat, 128), 1).astype(f32)) & (slot_of((flat, 128)) < capacity)
    member = jnp.where(match, 1.0, 0.0).astype(bf16)
    member_ref[...] = member
    grads = jnp.concatenate(
        [grad_ref[...], jnp.zeros((128 - bag_count, width), f32)], axis=0
    ).astype(bf16)
    rows = rows_ref[...]
    high = (rows >> 6).astype(f32).astype(bf16)
    low = (rows & 63).astype(f32).astype(bf16)
    lane = iota((capacity, width), 1)
    sub = iota((capacity, width), 0)
    meta = dot(high, jnp.where(lane == sub, 1.0, 0.0).astype(bf16)) + dot(
        low, jnp.where(lane == sub + 128, 1.0, 0.0).astype(bf16)
    )
    at_meta = jnp.where(slot_of((flat, shards)) == capacity, spread, 0.0).astype(bf16)
    out_ref[...] = (dot(member, grads) + dot(at_meta, meta.astype(bf16))).astype(bf16)


def prep(rows, bags, counts, grad):
    shards, capacity = rows.shape
    flat = shards * block
    return pl.pallas_call(
        prep_kernel,
        out_shape=(
            jax.ShapeDtypeStruct((flat, grad.shape[1]), bf16),
            jax.ShapeDtypeStruct((flat, 128), bf16),
        ),
        compiler_params=params,
        name="prep",
    )(rows, bags, counts, grad)


def hits_kernel(capacity, got_ref, listed_ref, part_ref, hits_ref):
    flat, width = got_ref.shape
    shards = flat // block
    touch = listed_ref.shape[1]
    got = got_ref[...]
    pick_shape = (shards, flat)
    pick = jnp.where(
        iota(pick_shape, 1) == block * iota(pick_shape, 0) + capacity, 1.0, 0.0
    ).astype(bf16)
    meta = dot(pick, got).astype(bf16)
    per_row = dot(spread_matrix(shards).astype(bf16), meta)
    own = (iota((flat, width), 1) & 127) == slot_of((flat, width))
    weigh = jnp.where(iota((width, 128), 0) < 128, 64.0, 1.0).astype(bf16)
    row = dot(jnp.where(own, per_row, 0.0).astype(bf16), weigh)
    row = jnp.where(slot_of((flat, 128)) < capacity, row, -1.0)
    for k in range(touch // 128):
        listed = listed_ref[:, k * 128 : (k + 1) * 128].astype(f32)
        hits_ref[:, k * 128 : (k + 1) * 128] = jnp.where(row == listed, 1.0, 0.0).astype(bf16)
    part_ref[...] = lax.dot_general(
        hits_ref[...], got, (((0,), (0,)), ((), ())), preferred_element_type=f32
    ).astype(bf16)


def find_hits(got, listed, capacity):
    flat, width = got.shape
    touch = listed.shape[1]
    return pl.pallas_call(
        functools.partial(hits_kernel, capacity),
        out_shape=(
            jax.ShapeDtypeStruct((touch, width), bf16),
            jax.ShapeDtypeStruct((flat, touch), bf16),
        ),
        compiler_params=params,
        name="hits",
    )(got, listed)


def pick_kernel(hits_ref, values_ref, out_ref):
    out_ref[...] = dot(hits_ref[...], values_ref[...]).astype(bf16)


def pick_rows(hits, values):
    return pl.pallas_call(
        pick_kernel,
        out_shape=jax.ShapeDtypeStruct((hits.shape[0], values.shape[1]), bf16),
        compiler_params=params,
        name="pick",
    )(hits, values)


def update_kernel(offset_ref, parts_ref, previous_ref, state_ref, out_ref):
    replicas, mine, width = parts_ref.shape
    grad = parts_ref[0].astype(f32)
    for k in range(1, replicas):
        grad = grad + parts_ref[k].astype(f32)
    grad = grad / replicas
    state = state_ref[...] + jnp.mean(grad * grad, axis=1, keepdims=True)
    out_ref[0:mine, :] = (
        previous_ref[...].astype(f32) - learn_rate * grad / (jnp.sqrt(state) + epsilon)
    ).astype(bf16)
    shape = (mine, width)
    at = iota(shape, 1) == iota(shape, 0) + offset_ref[0]
    line = jnp.sum(jnp.where(at, state, 0.0), axis=0, keepdims=True)
    first = line.astype(bf16).astype(f32)
    second = (line - first).astype(bf16).astype(f32)
    third = line - first - second
    sub = iota((16, width), 0)
    out_ref[mine : mine + 16, :] = jnp.where(
        sub == 0, first, jnp.where(sub == 1, second, jnp.where(sub == 2, third, 0.0))
    ).astype(bf16)


def update_rows(offset, parts, previous, state):
    _, mine, width = parts.shape
    vmem = pl.BlockSpec(memory_space=pltpu.VMEM)
    return pl.pallas_call(
        update_kernel,
        out_shape=jax.ShapeDtypeStruct((mine + 16, width), bf16),
        in_specs=[pl.BlockSpec(memory_space=pltpu.SMEM), vmem, vmem, vmem],
        compiler_params=params,
        name="update",
    )(offset, parts, previous, state)


def place_kernel(mine, every_ref, listed_ref, table_ref, state_ref, out_ref, state_out, values):
    step = pl.program_id(0)
    rows, width = table_ref.shape
    touch = listed_ref.shape[1]
    replicas = touch // mine
    stride = mine + 16

    @pl.when(step == 0)
    def _():
        for k in range(replicas):
            values[k * mine : (k + 1) * mine, :] = every_ref[k * stride : k * stride + mine, :]
        group = width // mine
        pieces = []
        for q in range(replicas // group):
            total = jnp.zeros((16, width), f32)
            for k in range(q * group, (q + 1) * group):
                total = total + every_ref[k * stride + mine : (k + 1) * stride, :].astype(f32)
            pieces.append(total)
        lines = jnp.concatenate(pieces, axis=1)
        high = state_ref.shape[0]
        listed = listed_ref[...]
        at_high = iota((high, touch), 0) == (listed >> 7)
        spread = jnp.concatenate(
            [jnp.where(at_high, lines[k : k + 1, :], 0.0) for k in range(3)], axis=0
        ).astype(bf16)
        at_low = jnp.where(iota((128, touch), 0) == (listed & 127), 1.0, 0.0).astype(bf16)
        placed = lax.dot_general(
            spread, at_low, (((1,), (1,)), ((), ())), preferred_element_type=f32
        )
        state_out[...] = state_ref[...] + (
            placed[0:high] + placed[high : 2 * high] + placed[2 * high : 3 * high]
        )

    row = (iota((rows, 128), 0) + step * rows).astype(f32)
    chosen = jnp.concatenate(
        [
            jnp.where(
                row == listed_ref[:, k * 128 : (k + 1) * 128].astype(f32), 1.0, 0.0
            ).astype(bf16)
            for k in range(touch // 128)
        ],
        axis=1,
    )
    out_ref[...] = (table_ref[...].astype(f32) + dot(chosen, values[...])).astype(bf16)


def place_rows(every, listed, table, state, mine):
    rows, width = table.shape
    touch = listed.shape[1]
    tile = 512
    high = rows // 128
    return pl.pallas_call(
        functools.partial(place_kernel, mine),
        grid=(rows // tile,),
        in_specs=[
            pl.BlockSpec(every.shape, lambda i: (0, 0)),
            pl.BlockSpec(listed.shape, lambda i: (0, 0)),
            pl.BlockSpec((tile, width), lambda i: (i, 0)),
            pl.BlockSpec((high, 128), lambda i: (0, 0)),
        ],
        out_specs=(
            pl.BlockSpec((tile, width), lambda i: (i, 0)),
            pl.BlockSpec((high, 128), lambda i: (0, 0)),
        ),
        out_shape=(
            jax.ShapeDtypeStruct((rows, width), bf16),
            jax.ShapeDtypeStruct((high, 128), f32),
        ),
        scratch_shapes=[pltpu.VMEM((touch, width), bf16)],
        compiler_params=params,
        name="place",
    )(every, listed, table, state.reshape(high, 128))


def pool_kernel(member_ref, rows_ref, out_ref):
    total = lax.dot_general(
        member_ref[...], rows_ref[...], (((0,), (0,)), ((), ())), preferred_element_type=f32
    )
    out_ref[...] = total[0 : out_ref.shape[0], :]


def pool_rows(member, rows, bag_count):
    return pl.pallas_call(
        pool_kernel,
        out_shape=jax.ShapeDtypeStruct((bag_count, rows.shape[1]), f32),
        compiler_params=params,
        name="pool",
    )(member, rows)


def local(table, row_state, touched_rows, lookup_rows, lookup_bags, route_counts, pooled_grad):
    shards = lax.axis_size("shard")
    replicas = lax.axis_size("replica")
    capacity = lookup_rows.shape[2]
    bag_count, width = pooled_grad.shape
    touch = touched_rows.shape[0]
    mine = touch // replicas
    listed = touched_rows.reshape(1, touch)

    send, member = prep(lookup_rows[0], lookup_bags[0], route_counts, pooled_grad)
    got = lax.all_to_all(
        send.reshape(shards, block, width), "shard", split_axis=0, concat_axis=0, tiled=True
    ).reshape(shards * block, width)

    replica = lax.axis_index("replica")
    values = jnp.take(table, touched_rows, axis=0, mode="clip")
    mine_values = lax.dynamic_slice(values, (replica * mine, 0), (mine, width))
    mine_rows = lax.dynamic_slice(touched_rows, (replica * mine,), (mine,))
    mine_state = jnp.take(row_state, mine_rows, mode="clip")[:, None]
    marked = jnp.zeros(row_state.shape, f32).at[touched_rows].set(
        1.0, mode="promise_in_bounds", unique_indices=True
    )
    kept_state = jnp.where(marked > 0, 0.0, row_state)
    kept_table = jnp.where(marked[:, None] > 0, jnp.zeros((), bf16), table)

    part, hits = find_hits(got, listed, capacity)
    parts = lax.all_to_all(
        part.reshape(replicas, mine, width), "replica", split_axis=0, concat_axis=0, tiled=True
    )
    picked = pick_rows(hits, values)
    offset = (lax.rem(replica, width // mine) * mine).astype(jnp.int32).reshape(1)
    updated = update_rows(offset, parts, mine_values, mine_state)
    picked, updated = lax.optimization_barrier((picked, updated))
    returned = lax.all_to_all(
        picked.reshape(shards, block, width), "shard", split_axis=0, concat_axis=0, tiled=True
    ).reshape(shards * block, width)
    every = lax.all_gather(updated, "replica", axis=0, tiled=True)
    new_table, new_state = place_rows(every, listed, kept_table, kept_state, mine)
    pooled = pool_rows(member, returned, bag_count)
    return (pooled, new_table, new_state.reshape(row_state.shape))


def solution(mesh):
    return jax.shard_map(
        local,
        mesh=mesh,
        in_specs=(
            P("shard", None),
            P("shard"),
            P("shard"),
            P("replica", "shard", None),
            P("replica", "shard", None),
            P("replica", "shard"),
            P(("replica", "shard"), None),
        ),
        out_specs=(P(("replica", "shard"), None), P("shard", None), P("shard")),
        check_vma=False,
    )
```

```python
import functools

import jax
import jax.numpy as jnp
from jax import lax
from jax.experimental import pallas as pl
from jax.experimental.pallas import tpu as pltpu
from jax.sharding import PartitionSpec as P

learn_rate = 0.5
epsilon = 1e-08
bf16 = jnp.bfloat16
f32 = jnp.float32

block = 24
dead = 200
large = pltpu.CompilerParams(vmem_limit_bytes=60 * 1024 * 1024)
params = pltpu.CompilerParams(vmem_limit_bytes=24 * 1024 * 1024)


def iota(shape, axis):
    return lax.broadcasted_iota(jnp.int32, shape, axis)


def dot(a, b):
    return jnp.dot(a, b, preferred_element_type=f32)


def pair_of(position):
    return (position * 2731) >> 16


def slot_of(shape):
    position = iota(shape, 0)
    return position - block * pair_of(position)


def spread_matrix(shards):
    shape = (shards * block, shards)
    return jnp.where(pair_of(iota(shape, 0)) == iota(shape, 1), 1.0, 0.0)


def keys_of(bags_ref, counts_ref):
    capacity, _, shards = bags_ref.shape
    bags = bags_ref[...].reshape(capacity, shards)
    live = iota((capacity, shards), 0) < counts_ref[...]
    return jnp.where(live, bags, dead).astype(f32).astype(bf16)


def dot_nt(a, b):
    return lax.dot_general(a, b, (((1,), (1,)), ((), ())), preferred_element_type=f32)


def dot_tn(a, b):
    return lax.dot_general(a, b, (((0,), (0,)), ((), ())), preferred_element_type=f32)


def prep_kernel(rows_ref, bags_ref, counts_ref, grad_ref, out_ref, held, sems):
    capacity, _, shards = rows_ref.shape
    bag_count, width = grad_ref.shape
    flat = shards * block
    key = keys_of(bags_ref, counts_ref)
    spread = spread_matrix(shards)
    per_row = dot_nt(spread.astype(bf16), key)
    own = slot_of((flat, capacity)) == iota((flat, capacity), 1)
    bag = dot(jnp.where(own, per_row, 0.0).astype(bf16), jnp.ones((capacity, 128), bf16))
    match = (bag == iota((flat, 128), 1).astype(f32)) & (slot_of((flat, 128)) < capacity)
    member = jnp.where(match, 1.0, 0.0).astype(bf16)
    grads = jnp.concatenate(
        [grad_ref[...], jnp.zeros((128 - bag_count, width), f32)], axis=0
    ).astype(bf16)
    rows = rows_ref[...].reshape(capacity, shards)
    high = (rows >> 6).astype(f32).astype(bf16)
    low = (rows & 63).astype(f32).astype(bf16)
    lane = iota((width, capacity), 0)
    sub = iota((width, capacity), 1)
    meta = dot(jnp.where(lane == sub, 1.0, 0.0).astype(bf16), high) + dot(
        jnp.where(lane == sub + 128, 1.0, 0.0).astype(bf16), low
    )
    at_meta = jnp.where(slot_of((flat, shards)) == capacity, spread, 0.0).astype(bf16)
    meta = meta.astype(bf16)
    pieces = sems.shape[0]
    size = flat // pieces
    copies = []
    for k in range(pieces):
        here = slice(k * size, (k + 1) * size)
        held[here, :] = (dot(member[here], grads) + dot_nt(at_meta[here], meta)).astype(bf16)
        at = pl.ds(k * size, size)
        copies.append(pltpu.make_async_copy(held.at[at], out_ref.at[at], sems.at[k]))
        copies[-1].start()
    for copy in copies:
        copy.wait()


def prep(rows, bags, counts, grad):
    shards = rows.shape[2]
    return pl.pallas_call(
        prep_kernel,
        out_shape=jax.ShapeDtypeStruct((shards * block, grad.shape[1]), bf16),
        out_specs=pl.BlockSpec(memory_space=pltpu.HBM),
        scratch_shapes=[
            pltpu.VMEM((shards * block, grad.shape[1]), bf16),
            pltpu.SemaphoreType.DMA((4,)),
        ],
        compiler_params=large,
        name="prep",
    )(rows, bags, counts, grad)


def packed_slot(position, capacity):
    whole = 16
    rest = capacity - whole
    tail = position - 2 * whole
    right = ((position >= whole) & (position < 2 * whole)) | (tail >= rest)
    slot = jnp.where(
        position < 2 * whole,
        position & (whole - 1),
        whole + jnp.where(tail >= rest, tail - rest, tail),
    )
    return slot, right


def member_kernel(bags_ref, counts_ref, out_ref):
    capacity, _, shards = bags_ref.shape
    pack = 2 * capacity
    flat = shards * pack
    key = keys_of(bags_ref, counts_ref)

    def pair_and_place(shape):
        row = iota(shape, 0)
        pair = (row * 13108) >> 19
        return pair, row - pack * pair

    shape = (flat, shards)
    spread = jnp.where(pair_and_place(shape)[0] == iota(shape, 1), 1.0, 0.0).astype(bf16)
    per_row = dot_nt(spread, key)
    shape = (flat, capacity)
    slot, _ = packed_slot(pair_and_place(shape)[1], capacity)
    own = jnp.where(slot == iota(shape, 1), per_row, 0.0).astype(bf16)
    bag = dot(own, jnp.ones((capacity, 128), bf16))
    shape = (flat, 128)
    _, right = packed_slot(pair_and_place(shape)[1], capacity)
    bag = bag + jnp.where(right, 64.0, 0.0)
    out_ref[...] = jnp.where(bag == iota(shape, 1).astype(f32), 1.0, 0.0).astype(bf16)


def member_matrix(bags, counts):
    capacity, _, shards = bags.shape
    return pl.pallas_call(
        member_kernel,
        out_shape=jax.ShapeDtypeStruct((shards * 2 * capacity, 128), bf16),
        compiler_params=params,
        name="member",
    )(bags, counts)


def sort_kernel(line_ref, column_ref, line_out):
    touch = line_ref.shape[1]
    tiles = touch // 128
    column = jnp.broadcast_to(column_ref[...], (touch, 128))
    lanes = iota((touch, 128), 1).astype(f32)
    below = jnp.zeros((touch, 128), f32)
    for k in range(tiles):
        line = line_ref[:, k * 128 : (k + 1) * 128]
        below = below + jnp.where(line < column, 1.0, 0.0)
    rank_column = jnp.sum(below, axis=1, keepdims=True)
    for k in range(tiles):
        at = rank_column == lanes + 128.0 * k
        line_out[:, k * 128 : (k + 1) * 128] = jnp.sum(
            jnp.where(at, column, 0.0), axis=0, keepdims=True
        ).astype(jnp.int32)


def sort_list(touched):
    touch = touched.shape[0]
    values = touched.astype(f32)
    return pl.pallas_call(
        sort_kernel,
        out_shape=jax.ShapeDtypeStruct((1, touch), jnp.int32),
        compiler_params=params,
        name="sort",
    )(values.reshape(1, touch), values.reshape(touch, 1))


def hit_matrix(got_ref, column_ref, hits, capacity):
    flat, width = got_ref.shape
    shards = flat // block
    column = column_ref[...]
    got = got_ref[...]
    meta = got.astype(f32).reshape(shards, block, width)[:, capacity : capacity + 1, :]
    shape = (shards, block, width)
    own = (iota(shape, 2) & 127) == iota(shape, 1)
    spread = jnp.where(own, jnp.broadcast_to(meta, shape), 0.0).reshape(flat, width).astype(bf16)
    weigh = jnp.where(iota((8, width), 1) < 128, 64.0, 1.0).astype(bf16)
    rows = dot_nt(weigh, spread)
    lane = iota((8, flat), 1)
    rows = jnp.where(lane - block * pair_of(lane) < capacity, rows, -1.0)
    for k in range(flat // 128):
        line = rows[0:1, k * 128 : (k + 1) * 128]
        hits[:, k * 128 : (k + 1) * 128] = jnp.where(column == line, 1.0, 0.0).astype(bf16)
    return got


def hits_kernel(capacity, got_ref, column_ref, hits_ref):
    hit_matrix(got_ref, column_ref, hits_ref, capacity)


def find_hits(got, column, capacity):
    flat, width = got.shape
    touch = column.shape[0]
    return pl.pallas_call(
        functools.partial(hits_kernel, capacity),
        out_shape=jax.ShapeDtypeStruct((touch, flat), bf16),
        compiler_params=params,
        name="hits",
    )(got, column)


def pick_kernel(hits, values_ref, out_ref):
    shards, pack, half = out_ref.shape
    whole = 16
    rest = pack // 2 - whole
    rows = dot_tn(hits[...], values_ref[...]).reshape(shards, block, 2 * half)
    left, right = rows[:, :, 0:half], rows[:, :, half : 2 * half]
    first = iota((shards, block - whole, half), 1) < rest
    mixed = jnp.where(
        first, left[:, whole:block, :], pltpu.roll(right[:, whole:block, :], rest, 1)
    )
    out_ref[...] = jnp.concatenate(
        [left[:, 0:whole, :], right[:, 0:whole, :], mixed], axis=1
    ).astype(bf16)


def pick_rows(hits, values, shards, capacity):
    return pl.pallas_call(
        pick_kernel,
        out_shape=jax.ShapeDtypeStruct((shards, 2 * capacity, values.shape[1] // 2), bf16),
        compiler_params=params,
        name="pick",
    )(hits, values)


def update_kernel(offset_ref, parts_ref, previous_ref, state_ref, out_ref):
    replicas, mine, width = parts_ref.shape
    grad = parts_ref[0].astype(f32)
    for k in range(1, replicas):
        grad = grad + parts_ref[k].astype(f32)
    grad = grad / replicas
    state = state_ref[...] + jnp.mean(grad * grad, axis=1, keepdims=True)
    out_ref[0:mine, :] = (
        previous_ref[...].astype(f32) - learn_rate * grad / (jnp.sqrt(state) + epsilon)
    ).astype(bf16)
    shape = (mine, width)
    at = iota(shape, 1) == iota(shape, 0) + offset_ref[0]
    line = jnp.sum(jnp.where(at, state, 0.0), axis=0, keepdims=True)
    first = line.astype(bf16).astype(f32)
    second = (line - first).astype(bf16).astype(f32)
    third = line - first - second
    sub = iota((16, width), 0)
    out_ref[mine : mine + 16, :] = jnp.where(
        sub == 0, first, jnp.where(sub == 1, second, jnp.where(sub == 2, third, 0.0))
    ).astype(bf16)


def update_rows(offset, parts, previous, state):
    _, mine, width = parts.shape
    vmem = pl.BlockSpec(memory_space=pltpu.VMEM)
    return pl.pallas_call(
        update_kernel,
        out_shape=jax.ShapeDtypeStruct((mine + 16, width), bf16),
        in_specs=[pl.BlockSpec(memory_space=pltpu.SMEM), vmem, vmem, vmem],
        compiler_params=params,
        name="update",
    )(offset, parts, previous, state)


def place_kernel(
    mine, starts, every_ref, listed_ref, tiles_ref, table_ref, state_ref, out_ref, state_out, values
):
    step = pl.program_id(0)
    rows, width = table_ref.shape
    touch = listed_ref.shape[1]
    replicas = touch // mine
    stride = mine + 16

    @pl.when(step == 0)
    def _():
        values[touch:, :] = jnp.zeros((256, width), bf16)
        for k in range(replicas):
            values[k * mine : (k + 1) * mine, :] = every_ref[k * stride : k * stride + mine, :]
        group = width // mine
        pieces = []
        for q in range(replicas // group):
            lines = jnp.zeros((16, width), f32)
            for k in range(q * group, (q + 1) * group):
                lines = lines + every_ref[k * stride + mine : (k + 1) * stride, :].astype(f32)
            pieces.append(lines)
        lines = jnp.concatenate(pieces, axis=1)
        high = state_ref.shape[0]
        listed = listed_ref[...]
        at_high = iota((high, touch), 0) == (listed >> 7)
        spread = jnp.concatenate(
            [jnp.where(at_high, lines[k : k + 1, :], 0.0) for k in range(3)], axis=0
        ).astype(bf16)
        at_low = jnp.where(iota((128, touch), 0) == (listed & 127), 1.0, 0.0).astype(bf16)
        placed = dot_nt(spread, at_low)
        state_out[...] = state_ref[...] + (
            placed[0:high] + placed[high : 2 * high] + placed[2 * high : 3 * high]
        )

    for k in range(rows // 128):
        at = step * (rows // 128) + k
        tile = starts[at] >> 7
        row = iota((128, 128), 0) + at * 128
        chosen = jnp.concatenate(
            [
                jnp.where(row == tiles_ref[pl.ds(tile + n, 1), :], 1.0, 0.0).astype(bf16)
                for n in range(2)
            ],
            axis=1,
        )
        window = values[pl.ds(pl.multiple_of(tile * 128, 128), 256), :]
        here = slice(k * 128, (k + 1) * 128)
        out_ref[here, :] = (table_ref[here, :].astype(f32) + dot(chosen, window)).astype(bf16)


def place_rows(starts, every, listed, table, state, mine, tile):
    rows, width = table.shape
    touch = listed.shape[1]
    high = rows // 128
    tiles = jnp.pad(listed.reshape(touch // 128, 128), ((0, 8), (0, 0)), constant_values=-1)
    whole = lambda i, starts: (0, 0)
    return pl.pallas_call(
        functools.partial(place_kernel, mine),
        grid_spec=pltpu.PrefetchScalarGridSpec(
            num_scalar_prefetch=1,
            grid=(rows // tile,),
            in_specs=[
                pl.BlockSpec(every.shape, whole),
                pl.BlockSpec(listed.shape, whole),
                pl.BlockSpec(tiles.shape, whole),
                pl.BlockSpec((tile, width), lambda i, starts: (i, 0)),
                pl.BlockSpec((high, 128), whole),
            ],
            out_specs=(
                pl.BlockSpec((tile, width), lambda i, starts: (i, 0)),
                pl.BlockSpec((high, 128), whole),
            ),
            scratch_shapes=[pltpu.VMEM((touch + 256, width), bf16)],
        ),
        out_shape=(
            jax.ShapeDtypeStruct((rows, width), bf16),
            jax.ShapeDtypeStruct((high, 128), f32),
        ),
        compiler_params=params,
        name="place",
    )(starts, every, listed, tiles, table, state.reshape(high, 128))


def pool_kernel(member_ref, rows_ref, out_ref):
    shards, pack, half = rows_ref.shape
    bag_count = out_ref.shape[0]
    rows = rows_ref[...].astype(f32).reshape(shards * pack, half).astype(bf16)
    total = dot_tn(member_ref[...], rows)
    out_ref[...] = jnp.concatenate([total[0:bag_count], total[64 : 64 + bag_count]], axis=1)


def pool_rows(member, rows, bag_count):
    return pl.pallas_call(
        pool_kernel,
        out_shape=jax.ShapeDtypeStruct((bag_count, 2 * rows.shape[2]), f32),
        compiler_params=params,
        name="pool",
    )(member, rows)


def local(table, row_state, touched_rows, lookup_rows, lookup_bags, route_counts, pooled_grad):
    shards = lax.axis_size("shard")
    replicas = lax.axis_size("replica")
    capacity = lookup_rows.shape[2]
    bag_count, width = pooled_grad.shape
    touch = touched_rows.shape[0]
    mine = touch // replicas
    rows = row_state.shape[0]
    tile = 1024

    bags = jnp.transpose(lookup_bags, (2, 0, 1))
    send = prep(jnp.transpose(lookup_rows, (2, 0, 1)), bags, route_counts, pooled_grad)
    got = lax.all_to_all(
        send.reshape(shards, block, width), "shard", split_axis=0, concat_axis=0, tiled=True
    ).reshape(shards * block, width)

    listed = sort_list(touched_rows)
    column = jnp.broadcast_to(listed.reshape(touch, 1).astype(f32), (touch, 128))
    order = listed.reshape(touch)
    bounds = jnp.arange(rows // 128, dtype=jnp.int32) * 128
    starts = jnp.sum((touched_rows[None, :] < bounds[:, None]).astype(jnp.int32), axis=1)
    replica = lax.axis_index("replica")
    values = jnp.take(table, order, axis=0, mode="clip")
    mine_values = lax.dynamic_slice(values, (replica * mine, 0), (mine, width))
    mine_rows = lax.dynamic_slice(order, (replica * mine,), (mine,))
    mine_state = jnp.take(row_state, mine_rows, mode="clip")[:, None]
    marked = jnp.zeros(row_state.shape, f32).at[touched_rows].set(
        1.0, mode="promise_in_bounds", unique_indices=True
    )
    kept_state = jnp.where(marked > 0, 0.0, row_state)
    kept_table = jnp.where(marked[:, None] > 0, jnp.zeros((), bf16), table)
    got, column, kept_state, kept_table, mine_state, mine_values, starts = (
        lax.optimization_barrier(
            (got, column, kept_state, kept_table, mine_state, mine_values, starts)
        )
    )

    hits = find_hits(got, column, capacity)
    part = dot(hits, got).astype(bf16)
    parts = lax.all_to_all(
        part.reshape(replicas, mine, width), "replica", split_axis=0, concat_axis=0, tiled=True
    )
    picked = pick_rows(hits, values, shards, capacity)
    member = member_matrix(bags, route_counts)
    offset = (lax.rem(replica, width // mine) * mine).astype(jnp.int32).reshape(1)
    updated = update_rows(offset, parts, mine_values, mine_state)
    picked, member, updated = lax.optimization_barrier((picked, member, updated))
    returned = lax.all_to_all(picked, "shard", split_axis=0, concat_axis=0, tiled=True)
    every = lax.all_gather(updated, "replica", axis=0, tiled=True)
    new_table, new_state = place_rows(starts, every, listed, kept_table, kept_state, mine, tile)
    pooled = pool_rows(member, returned, bag_count)
    return (pooled, new_table, new_state.reshape(row_state.shape))


def solution(mesh):
    return jax.shard_map(
        local,
        mesh=mesh,
        in_specs=(
            P("shard", None),
            P("shard"),
            P("shard"),
            P("replica", "shard", None),
            P("replica", "shard", None),
            P("replica", "shard"),
            P(("replica", "shard"), None),
        ),
        out_specs=(P(("replica", "shard"), None), P("shard", None), P("shard")),
        check_vma=False,
    )
```

```python
import functools

import jax
import jax.numpy as jnp
from jax import lax
from jax.experimental import pallas as pl
from jax.experimental.pallas import tpu as pltpu
from jax.sharding import PartitionSpec as P

learn_rate = 0.5
epsilon = 1e-08
bf16 = jnp.bfloat16
f32 = jnp.float32

block = 24
dead = 200
large = pltpu.CompilerParams(vmem_limit_bytes=60 * 1024 * 1024)
params = pltpu.CompilerParams(vmem_limit_bytes=24 * 1024 * 1024)


def iota(shape, axis):
    return lax.broadcasted_iota(jnp.int32, shape, axis)


def dot(a, b):
    return jnp.dot(a, b, preferred_element_type=f32)


def pair_of(position):
    return (position * 2731) >> 16


def slot_of(shape):
    position = iota(shape, 0)
    return position - block * pair_of(position)


def spread_matrix(shards):
    shape = (shards * block, shards)
    return jnp.where(pair_of(iota(shape, 0)) == iota(shape, 1), 1.0, 0.0)


def keys_of(bags_ref, counts_ref):
    capacity, _, shards = bags_ref.shape
    bags = bags_ref[...].reshape(capacity, shards)
    live = iota((capacity, shards), 0) < counts_ref[...]
    return jnp.where(live, bags, dead).astype(f32).astype(bf16)


def dot_nt(a, b):
    return lax.dot_general(a, b, (((1,), (1,)), ((), ())), preferred_element_type=f32)


def dot_tn(a, b):
    return lax.dot_general(a, b, (((0,), (0,)), ((), ())), preferred_element_type=f32)


def prep_kernel(rows_ref, bags_ref, counts_ref, grad_ref, out_ref, held, sems):
    capacity, _, shards = rows_ref.shape
    bag_count, width = grad_ref.shape
    flat = shards * block
    key = keys_of(bags_ref, counts_ref)
    spread = spread_matrix(shards)
    per_row = dot_nt(spread.astype(bf16), key)
    own = slot_of((flat, capacity)) == iota((flat, capacity), 1)
    bag = dot(jnp.where(own, per_row, 0.0).astype(bf16), jnp.ones((capacity, 128), bf16))
    match = (bag == iota((flat, 128), 1).astype(f32)) & (slot_of((flat, 128)) < capacity)
    member = jnp.where(match, 1.0, 0.0).astype(bf16)
    grads = jnp.concatenate(
        [grad_ref[...], jnp.zeros((128 - bag_count, width), f32)], axis=0
    ).astype(bf16)
    rows = rows_ref[...].reshape(capacity, shards)
    high = (rows >> 6).astype(f32).astype(bf16)
    low = (rows & 63).astype(f32).astype(bf16)
    lane = iota((width, capacity), 0)
    sub = iota((width, capacity), 1)
    meta = dot(jnp.where(lane == sub, 1.0, 0.0).astype(bf16), high) + dot(
        jnp.where(lane == sub + 128, 1.0, 0.0).astype(bf16), low
    )
    at_meta = jnp.where(slot_of((flat, shards)) == capacity, spread, 0.0).astype(bf16)
    meta = meta.astype(bf16)
    pieces = sems.shape[0]
    size = flat // pieces
    copies = []
    for k in range(pieces):
        here = slice(k * size, (k + 1) * size)
        held[here, :] = (dot(member[here], grads) + dot_nt(at_meta[here], meta)).astype(bf16)
        at = pl.ds(k * size, size)
        copies.append(pltpu.make_async_copy(held.at[at], out_ref.at[at], sems.at[k]))
        copies[-1].start()
    for copy in copies:
        copy.wait()


def prep(rows, bags, counts, grad):
    shards = rows.shape[2]
    return pl.pallas_call(
        prep_kernel,
        out_shape=jax.ShapeDtypeStruct((shards * block, grad.shape[1]), bf16),
        out_specs=pl.BlockSpec(memory_space=pltpu.HBM),
        scratch_shapes=[
            pltpu.VMEM((shards * block, grad.shape[1]), bf16),
            pltpu.SemaphoreType.DMA((4,)),
        ],
        compiler_params=large,
        name="prep",
    )(rows, bags, counts, grad)


def packed_slot(position, capacity):
    whole = 16
    rest = capacity - whole
    tail = position - 2 * whole
    right = ((position >= whole) & (position < 2 * whole)) | (tail >= rest)
    slot = jnp.where(
        position < 2 * whole,
        position & (whole - 1),
        whole + jnp.where(tail >= rest, tail - rest, tail),
    )
    return slot, right


def member_kernel(bags_ref, counts_ref, out_ref):
    capacity, _, shards = bags_ref.shape
    pack = 2 * capacity
    flat = shards * pack
    key = keys_of(bags_ref, counts_ref)

    def pair_and_place(shape):
        row = iota(shape, 0)
        pair = (row * 13108) >> 19
        return pair, row - pack * pair

    shape = (flat, shards)
    spread = jnp.where(pair_and_place(shape)[0] == iota(shape, 1), 1.0, 0.0).astype(bf16)
    per_row = dot_nt(spread, key)
    shape = (flat, capacity)
    slot, _ = packed_slot(pair_and_place(shape)[1], capacity)
    own = jnp.where(slot == iota(shape, 1), per_row, 0.0).astype(bf16)
    bag = dot(own, jnp.ones((capacity, 128), bf16))
    shape = (flat, 128)
    _, right = packed_slot(pair_and_place(shape)[1], capacity)
    bag = bag + jnp.where(right, 64.0, 0.0)
    out_ref[...] = jnp.where(bag == iota(shape, 1).astype(f32), 1.0, 0.0).astype(bf16)


def member_matrix(bags, counts):
    capacity, _, shards = bags.shape
    return pl.pallas_call(
        member_kernel,
        out_shape=jax.ShapeDtypeStruct((shards * 2 * capacity, 128), bf16),
        compiler_params=params,
        name="member",
    )(bags, counts)


def sort_kernel(line_ref, column_ref, line_out):
    touch = line_ref.shape[1]
    tiles = touch // 128
    column = jnp.broadcast_to(column_ref[...], (touch, 128))
    lanes = iota((touch, 128), 1).astype(f32)
    below = jnp.zeros((touch, 128), f32)
    for k in range(tiles):
        line = line_ref[:, k * 128 : (k + 1) * 128]
        below = below + jnp.where(line < column, 1.0, 0.0)
    rank_column = jnp.sum(below, axis=1, keepdims=True)
    for k in range(tiles):
        at = rank_column == lanes + 128.0 * k
        line_out[:, k * 128 : (k + 1) * 128] = jnp.sum(
            jnp.where(at, column, 0.0), axis=0, keepdims=True
        ).astype(jnp.int32)


def sort_list(touched):
    touch = touched.shape[0]
    values = touched.astype(f32)
    return pl.pallas_call(
        sort_kernel,
        out_shape=jax.ShapeDtypeStruct((1, touch), jnp.int32),
        compiler_params=params,
        name="sort",
    )(values.reshape(1, touch), values.reshape(touch, 1))


def hit_matrix(got_ref, column_ref, hits, capacity):
    flat, width = got_ref.shape
    shards = flat // block
    column = column_ref[...]
    got = got_ref[...]
    meta = got.astype(f32).reshape(shards, block, width)[:, capacity : capacity + 1, :]
    shape = (shards, block, width)
    own = (iota(shape, 2) & 127) == iota(shape, 1)
    spread = jnp.where(own, jnp.broadcast_to(meta, shape), 0.0).reshape(flat, width).astype(bf16)
    weigh = jnp.where(iota((8, width), 1) < 128, 64.0, 1.0).astype(bf16)
    rows = dot_nt(weigh, spread)
    lane = iota((8, flat), 1)
    rows = jnp.where(lane - block * pair_of(lane) < capacity, rows, -1.0)
    for k in range(flat // 128):
        line = rows[0:1, k * 128 : (k + 1) * 128]
        hits[:, k * 128 : (k + 1) * 128] = jnp.where(column == line, 1.0, 0.0).astype(bf16)
    return got


def hits_kernel(capacity, got_ref, column_ref, theirs_ref, ours_ref, hits):
    got = hit_matrix(got_ref, column_ref, hits, capacity)
    half = theirs_ref.shape[0]
    theirs_ref[...] = dot(hits[0:half, :], got).astype(bf16)
    ours_ref[...] = dot(hits[half:, :], got)


def partial_sums(got, column, capacity):
    flat, width = got.shape
    touch = column.shape[0]
    return pl.pallas_call(
        functools.partial(hits_kernel, capacity),
        out_shape=(
            jax.ShapeDtypeStruct((touch // 2, width), bf16),
            jax.ShapeDtypeStruct((touch // 2, width), f32),
        ),
        scratch_shapes=[pltpu.VMEM((touch, flat), bf16)],
        compiler_params=params,
        name="hits",
    )(got, column)


def pick_kernel(capacity, got_ref, column_ref, values_ref, out_ref, hits):
    hit_matrix(got_ref, column_ref, hits, capacity)
    shards, pack, half = out_ref.shape
    whole = 16
    rest = pack // 2 - whole
    rows = dot_tn(hits[...], values_ref[...]).reshape(shards, block, 2 * half)
    left, right = rows[:, :, 0:half], rows[:, :, half : 2 * half]
    first = iota((shards, block - whole, half), 1) < rest
    mixed = jnp.where(
        first, left[:, whole:block, :], pltpu.roll(right[:, whole:block, :], rest, 1)
    )
    out_ref[...] = jnp.concatenate(
        [left[:, 0:whole, :], right[:, 0:whole, :], mixed], axis=1
    ).astype(bf16)


def pick_rows(got, column, values, shards, capacity):
    return pl.pallas_call(
        functools.partial(pick_kernel, capacity),
        out_shape=jax.ShapeDtypeStruct((shards, 2 * capacity, values.shape[1] // 2), bf16),
        scratch_shapes=[pltpu.VMEM((values.shape[0], got.shape[0]), bf16)],
        compiler_params=params,
        name="pick",
    )(got, column, values)


def update_kernel(offset_ref, parts_ref, previous_ref, state_ref, out_ref):
    replicas, chunk, width = parts_ref.shape
    mine = 2 * chunk
    halves = []
    for core in range(2):
        total = parts_ref[core].astype(f32)
        for k in range(core + 2, replicas, 2):
            total = total + parts_ref[k].astype(f32)
        halves.append(total)
    grad = jnp.concatenate(halves, axis=0) / replicas
    state = state_ref[...] + jnp.mean(grad * grad, axis=1, keepdims=True)
    out_ref[0:mine, :] = (
        previous_ref[...].astype(f32) - learn_rate * grad / (jnp.sqrt(state) + epsilon)
    ).astype(bf16)
    at = iota((chunk, width), 1) == iota((chunk, width), 0) + offset_ref[0]
    sub = iota((16, width), 0)
    lines = jnp.zeros((16, width), f32)
    for core in range(2):
        own = state[core * chunk : (core + 1) * chunk]
        line = jnp.sum(jnp.where(at, own, 0.0), axis=0, keepdims=True)
        first = line.astype(bf16).astype(f32)
        second = (line - first).astype(bf16).astype(f32)
        for k, piece in enumerate((first, second, line - first - second)):
            lines = jnp.where(sub == 3 * core + k, piece, lines)
    out_ref[mine : mine + 16, :] = lines.astype(bf16)


def update_rows(offset, parts, previous, state):
    _, chunk, width = parts.shape
    mine = 2 * chunk
    vmem = pl.BlockSpec(memory_space=pltpu.VMEM)
    return pl.pallas_call(
        update_kernel,
        out_shape=jax.ShapeDtypeStruct((mine + 16, width), bf16),
        in_specs=[pl.BlockSpec(memory_space=pltpu.SMEM), vmem, vmem, vmem],
        compiler_params=params,
        name="update",
    )(offset, parts, previous, state)


def place_kernel(
    mine, starts, every_ref, listed_ref, tiles_ref, table_ref, state_ref, out_ref, state_out, values
):
    step = pl.program_id(0)
    rows, width = table_ref.shape
    touch = listed_ref.shape[1]
    replicas = touch // mine
    stride = mine + 16

    @pl.when(step == 0)
    def _():
        values[touch:, :] = jnp.zeros((256, width), bf16)
        chunk = mine // 2
        for k in range(replicas):
            for core in range(2):
                at = core * (touch // 2) + k * chunk
                source = k * stride + core * chunk
                values[at : at + chunk, :] = every_ref[source : source + chunk, :]
        group = width // chunk
        pieces = []
        for q in range(replicas // group):
            lines = jnp.zeros((16, width), f32)
            for k in range(q * group, (q + 1) * group):
                lines = lines + every_ref[k * stride + mine : (k + 1) * stride, :].astype(f32)
            pieces.append(lines)
        lines = jnp.concatenate(
            [lines[3 * core : 3 * core + 3] for core in range(2) for lines in pieces], axis=1
        )
        high = state_ref.shape[0]
        listed = listed_ref[...]
        at_high = iota((high, touch), 0) == (listed >> 7)
        spread = jnp.concatenate(
            [jnp.where(at_high, lines[k : k + 1, :], 0.0) for k in range(3)], axis=0
        ).astype(bf16)
        at_low = jnp.where(iota((128, touch), 0) == (listed & 127), 1.0, 0.0).astype(bf16)
        placed = dot_nt(spread, at_low)
        state_out[...] = state_ref[...] + (
            placed[0:high] + placed[high : 2 * high] + placed[2 * high : 3 * high]
        )

    for k in range(rows // 128):
        at = step * (rows // 128) + k
        tile = starts[at] >> 7
        row = iota((128, 128), 0) + at * 128
        chosen = jnp.concatenate(
            [
                jnp.where(row == tiles_ref[pl.ds(tile + n, 1), :], 1.0, 0.0).astype(bf16)
                for n in range(2)
            ],
            axis=1,
        )
        window = values[pl.ds(pl.multiple_of(tile * 128, 128), 256), :]
        here = slice(k * 128, (k + 1) * 128)
        out_ref[here, :] = (table_ref[here, :].astype(f32) + dot(chosen, window)).astype(bf16)


def place_rows(starts, every, listed, table, state, mine, tile):
    rows, width = table.shape
    touch = listed.shape[1]
    high = rows // 128
    tiles = jnp.pad(listed.reshape(touch // 128, 128), ((0, 8), (0, 0)), constant_values=-1)
    whole = lambda i, starts: (0, 0)
    return pl.pallas_call(
        functools.partial(place_kernel, mine),
        grid_spec=pltpu.PrefetchScalarGridSpec(
            num_scalar_prefetch=1,
            grid=(rows // tile,),
            in_specs=[
                pl.BlockSpec(every.shape, whole),
                pl.BlockSpec(listed.shape, whole),
                pl.BlockSpec(tiles.shape, whole),
                pl.BlockSpec((tile, width), lambda i, starts: (i, 0)),
                pl.BlockSpec((high, 128), whole),
            ],
            out_specs=(
                pl.BlockSpec((tile, width), lambda i, starts: (i, 0)),
                pl.BlockSpec((high, 128), whole),
            ),
            scratch_shapes=[pltpu.VMEM((touch + 256, width), bf16)],
        ),
        out_shape=(
            jax.ShapeDtypeStruct((rows, width), bf16),
            jax.ShapeDtypeStruct((high, 128), f32),
        ),
        compiler_params=params,
        name="place",
    )(starts, every, listed, tiles, table, state.reshape(high, 128))


def pool_kernel(member_ref, rows_ref, out_ref):
    shards, pack, half = rows_ref.shape
    bag_count = out_ref.shape[0]
    rows = rows_ref[...].astype(f32).reshape(shards * pack, half).astype(bf16)
    total = dot_tn(member_ref[...], rows)
    out_ref[...] = jnp.concatenate([total[0:bag_count], total[64 : 64 + bag_count]], axis=1)


def pool_rows(member, rows, bag_count):
    return pl.pallas_call(
        pool_kernel,
        out_shape=jax.ShapeDtypeStruct((bag_count, 2 * rows.shape[2]), f32),
        compiler_params=params,
        name="pool",
    )(member, rows)


def local(table, row_state, touched_rows, lookup_rows, lookup_bags, route_counts, pooled_grad):
    shards = lax.axis_size("shard")
    replicas = lax.axis_size("replica")
    capacity = lookup_rows.shape[2]
    bag_count, width = pooled_grad.shape
    touch = touched_rows.shape[0]
    mine = touch // replicas
    rows = row_state.shape[0]
    tile = 1024

    bags = jnp.transpose(lookup_bags, (2, 0, 1))
    send = prep(jnp.transpose(lookup_rows, (2, 0, 1)), bags, route_counts, pooled_grad)
    got = lax.all_to_all(
        send.reshape(shards, block, width), "shard", split_axis=0, concat_axis=0, tiled=True
    ).reshape(shards * block, width)

    listed = sort_list(touched_rows)
    replica = lax.axis_index("replica")
    half = touch // 2
    order = listed.reshape(touch)
    core = lax.rem(replica, 2)
    theirs = lax.dynamic_slice(order, ((1 - core) * half,), (half,))
    ours = lax.dynamic_slice(order, (core * half,), (half,))
    turned = jnp.concatenate([theirs, ours])
    column = jnp.broadcast_to(turned.reshape(touch, 1).astype(f32), (touch, 128))
    bounds = jnp.arange(rows // 128, dtype=jnp.int32) * 128
    starts = jnp.sum((touched_rows[None, :] < bounds[:, None]).astype(jnp.int32), axis=1)
    values = jnp.take(table, turned, axis=0, mode="clip")
    chunk = mine // 2
    mine_rows = lax.dynamic_slice(order.reshape(2, half), (0, replica * chunk), (2, chunk))
    mine_rows = mine_rows.reshape(mine)
    mine_values = jnp.take(table, mine_rows, axis=0, mode="clip")
    mine_state = jnp.take(row_state, mine_rows, mode="clip")[:, None]
    marked = jnp.zeros(row_state.shape, f32).at[touched_rows].set(
        1.0, mode="promise_in_bounds", unique_indices=True
    )
    kept_state = jnp.where(marked > 0, 0.0, row_state)
    kept_table = jnp.where(marked[:, None] > 0, jnp.zeros((), bf16), table)
    got, column, values, kept_state, kept_table, mine_state, mine_values, starts = (
        lax.optimization_barrier(
            (got, column, values, kept_state, kept_table, mine_state, mine_values, starts)
        )
    )

    theirs, ours = partial_sums(got, column, capacity)
    theirs = lax.ppermute(theirs, "replica", [(k, k ^ 1) for k in range(replicas)])
    part = (ours + theirs.astype(f32)).astype(bf16)
    parts = lax.all_to_all(
        part.reshape(replicas, chunk, width), "replica", split_axis=0, concat_axis=0, tiled=True
    )
    picked = pick_rows(got, column, values, shards, capacity)
    member = member_matrix(bags, route_counts)
    offset = (lax.rem(replica, width // chunk) * chunk).astype(jnp.int32).reshape(1)
    picked, member, parts = lax.optimization_barrier((picked, member, parts))
    returned = lax.all_to_all(picked, "shard", split_axis=0, concat_axis=0, tiled=True)
    updated = update_rows(offset, parts, mine_values, mine_state)
    every = lax.all_gather(updated, "replica", axis=0, tiled=True)
    new_table, new_state = place_rows(starts, every, listed, kept_table, kept_state, mine, tile)
    pooled = pool_rows(member, returned, bag_count)
    return (pooled, new_table, new_state.reshape(row_state.shape))


def solution(mesh):
    return jax.shard_map(
        local,
        mesh=mesh,
        in_specs=(
            P("shard", None),
            P("shard"),
            P("shard"),
            P("replica", "shard", None),
            P("replica", "shard", None),
            P("replica", "shard"),
            P(("replica", "shard"), None),
        ),
        out_specs=(P(("replica", "shard"), None), P("shard", None), P("shard")),
        check_vma=False,
    )
```

```python
import functools

import jax
import jax.numpy as jnp
from jax import lax
from jax.experimental import pallas as pl
from jax.experimental.pallas import tpu as pltpu
from jax.sharding import PartitionSpec as P

learn_rate = 0.5
epsilon = 1e-08
bf16 = jnp.bfloat16
f32 = jnp.float32

block = 24
dead = 200
large = pltpu.CompilerParams(vmem_limit_bytes=60 * 1024 * 1024)
params = pltpu.CompilerParams(vmem_limit_bytes=24 * 1024 * 1024)


def iota(shape, axis):
    return lax.broadcasted_iota(jnp.int32, shape, axis)


def dot(a, b):
    return jnp.dot(a, b, preferred_element_type=f32)


def pair_of(position):
    return (position * 2731) >> 16


def keys_of(bags_ref, counts_ref):
    capacity, _, shards = bags_ref.shape
    bags = bags_ref[...].reshape(capacity, shards)
    live = iota((capacity, shards), 0) < counts_ref[...]
    return jnp.where(live, bags, dead).astype(f32).astype(bf16)


def dot_nt(a, b):
    return lax.dot_general(a, b, (((1,), (1,)), ((), ())), preferred_element_type=f32)


def dot_tn(a, b):
    return lax.dot_general(a, b, (((0,), (0,)), ((), ())), preferred_element_type=f32)


def prep_kernel(rows_ref, bags_ref, counts_ref, grad_ref, out_ref, held, sems):
    capacity, _, shards = rows_ref.shape
    bag_count, width = grad_ref.shape
    flat = shards * block
    key = keys_of(bags_ref, counts_ref)
    position, lane = iota((flat, 128), 0), iota((flat, 128), 1)
    pair = pair_of(position)
    slot = position - block * pair
    spread = jnp.where(pair == lane, 1.0, 0.0)
    per_row = dot_nt(spread.astype(bf16)[:, 0:shards], key)
    per_row = jnp.where((slot == lane)[:, 0:capacity], per_row, 0.0).astype(bf16)
    bag = dot(per_row, jnp.ones((capacity, 128), bf16))
    bag = jnp.where(slot < capacity, bag, float(dead))
    member = jnp.where(bag == lane.astype(f32), 1.0, 0.0).astype(bf16)
    grads = jnp.concatenate(
        [grad_ref[...], jnp.zeros((128 - bag_count, width), f32)], axis=0
    ).astype(bf16)
    rows = rows_ref[...].reshape(capacity, shards)
    high = (rows >> 6).astype(f32).astype(bf16)
    low = (rows & 63).astype(f32).astype(bf16)
    lane = iota((width, capacity), 0)
    sub = iota((width, capacity), 1)
    meta = dot(jnp.where(lane == sub, 1.0, 0.0).astype(bf16), high) + dot(
        jnp.where(lane == sub + 128, 1.0, 0.0).astype(bf16), low
    )
    at_meta = jnp.where(slot == capacity, spread, 0.0).astype(bf16)[:, 0:shards]
    meta = meta.astype(bf16)
    pieces = sems.shape[0]
    size = flat // pieces
    copies = []
    for k in range(pieces):
        here = slice(k * size, (k + 1) * size)
        held[here, :] = (dot(member[here], grads) + dot_nt(at_meta[here], meta)).astype(bf16)
        at = pl.ds(k * size, size)
        copies.append(pltpu.make_async_copy(held.at[at], out_ref.at[at], sems.at[k]))
        copies[-1].start()
    for copy in copies:
        copy.wait()


def prep(rows, bags, counts, grad):
    shards = rows.shape[2]
    return pl.pallas_call(
        prep_kernel,
        out_shape=jax.ShapeDtypeStruct((shards * block, grad.shape[1]), bf16),
        out_specs=pl.BlockSpec(memory_space=pltpu.HBM),
        scratch_shapes=[
            pltpu.VMEM((shards * block, grad.shape[1]), bf16),
            pltpu.SemaphoreType.DMA((4,)),
        ],
        compiler_params=large,
        name="prep",
    )(rows, bags, counts, grad)


def packed_slot(position, capacity):
    whole = 16
    rest = capacity - whole
    tail = position - 2 * whole
    right = ((position >= whole) & (position < 2 * whole)) | (tail >= rest)
    slot = jnp.where(
        position < 2 * whole,
        position & (whole - 1),
        whole + jnp.where(tail >= rest, tail - rest, tail),
    )
    return slot, right


def member_kernel(bags_ref, counts_ref, out_ref):
    capacity, _, shards = bags_ref.shape
    pack = 2 * capacity
    flat = shards * pack
    key = keys_of(bags_ref, counts_ref)

    def pair_and_place(shape, axis):
        row = iota(shape, axis)
        pair = (row * 13108) >> 19
        return pair, row - pack * pair

    shape = (shards, flat)
    spread = jnp.where(pair_and_place(shape, 1)[0] == iota(shape, 0), 1.0, 0.0).astype(bf16)
    per_row = dot(key, spread)
    shape = (capacity, flat)
    slot, _ = packed_slot(pair_and_place(shape, 1)[1], capacity)
    own = jnp.where(slot == iota(shape, 0), per_row, 0.0).astype(bf16)
    bag = dot(jnp.ones((128, capacity), bf16), own)
    shape = (128, flat)
    _, right = packed_slot(pair_and_place(shape, 1)[1], capacity)
    bag = bag + jnp.where(right, 64.0, 0.0)
    out_ref[...] = jnp.where(bag == iota(shape, 0).astype(f32), 1.0, 0.0).astype(bf16)


def member_matrix(bags, counts):
    capacity, _, shards = bags.shape
    return pl.pallas_call(
        member_kernel,
        out_shape=jax.ShapeDtypeStruct((128, shards * 2 * capacity), bf16),
        compiler_params=params,
        name="member",
    )(bags, counts)


def sort_kernel(line_ref, column_ref, line_out):
    touch = line_ref.shape[1]
    tiles = touch // 128
    column = jnp.broadcast_to(column_ref[...], (touch, 128))
    lanes = iota((touch, 128), 1).astype(f32)
    below = jnp.zeros((touch, 128), f32)
    for k in range(tiles):
        line = line_ref[:, k * 128 : (k + 1) * 128]
        below = below + jnp.where(line < column, 1.0, 0.0)
    rank_column = jnp.sum(below, axis=1, keepdims=True)
    for k in range(tiles):
        at = rank_column == lanes + 128.0 * k
        line_out[:, k * 128 : (k + 1) * 128] = jnp.sum(
            jnp.where(at, column, 0.0), axis=0, keepdims=True
        ).astype(jnp.int32)


def sort_list(touched):
    touch = touched.shape[0]
    values = touched.astype(f32)
    return pl.pallas_call(
        sort_kernel,
        out_shape=jax.ShapeDtypeStruct((1, touch), jnp.int32),
        compiler_params=params,
        name="sort",
    )(values.reshape(1, touch), values.reshape(touch, 1))


def hit_matrix(got_ref, column_ref, hits, capacity):
    flat, width = got_ref.shape
    shards = flat // block
    column = column_ref[...]
    got = got_ref[...]
    meta = got.astype(f32).reshape(shards, block, width)[:, capacity : capacity + 1, :]
    shape = (shards, block, width)
    own = (iota(shape, 2) & 127) == iota(shape, 1)
    spread = jnp.where(own, jnp.broadcast_to(meta, shape), 0.0).reshape(flat, width).astype(bf16)
    weigh = jnp.where(iota((8, width), 1) < 128, 64.0, 1.0).astype(bf16)
    rows = dot_nt(weigh, spread)
    lane = iota((8, flat), 1)
    rows = jnp.where(lane - block * pair_of(lane) < capacity, rows, -1.0)
    for k in range(flat // 128):
        line = rows[0:1, k * 128 : (k + 1) * 128]
        hits[:, k * 128 : (k + 1) * 128] = jnp.where(column == line, 1.0, 0.0).astype(bf16)
    return got


def hits_kernel(capacity, got_ref, column_ref, theirs_ref, ours_ref, hits):
    got = hit_matrix(got_ref, column_ref, hits, capacity)
    half = theirs_ref.shape[0]
    theirs_ref[...] = dot(hits[0:half, :], got).astype(bf16)
    ours_ref[...] = dot(hits[half:, :], got)


def partial_sums(got, column, capacity):
    flat, width = got.shape
    touch = column.shape[0]
    return pl.pallas_call(
        functools.partial(hits_kernel, capacity),
        out_shape=(
            jax.ShapeDtypeStruct((touch // 2, width), bf16),
            jax.ShapeDtypeStruct((touch // 2, width), f32),
        ),
        scratch_shapes=[pltpu.VMEM((touch, flat), bf16)],
        compiler_params=params,
        name="hits",
    )(got, column)


def pick_kernel(capacity, got_ref, column_ref, values_ref, out_ref, hits):
    hit_matrix(got_ref, column_ref, hits, capacity)
    shards, pack, half = out_ref.shape
    whole = 16
    rest = pack // 2 - whole
    rows = dot_tn(hits[...], values_ref[...]).reshape(shards, block, 2 * half)
    left, right = rows[:, :, 0:half], rows[:, :, half : 2 * half]
    first = iota((shards, block - whole, half), 1) < rest
    mixed = jnp.where(
        first, left[:, whole:block, :], pltpu.roll(right[:, whole:block, :], rest, 1)
    )
    out_ref[...] = jnp.concatenate(
        [left[:, 0:whole, :], right[:, 0:whole, :], mixed], axis=1
    ).astype(bf16)


def pick_rows(got, column, values, shards, capacity):
    return pl.pallas_call(
        functools.partial(pick_kernel, capacity),
        out_shape=jax.ShapeDtypeStruct((shards, 2 * capacity, values.shape[1] // 2), bf16),
        scratch_shapes=[pltpu.VMEM((values.shape[0], got.shape[0]), bf16)],
        compiler_params=params,
        name="pick",
    )(got, column, values)


def update_kernel(offset_ref, parts_ref, previous_ref, state_ref, out_ref):
    replicas, chunk, width = parts_ref.shape
    mine = 2 * chunk
    halves = []
    for core in range(2):
        total = parts_ref[core].astype(f32)
        for k in range(core + 2, replicas, 2):
            total = total + parts_ref[k].astype(f32)
        halves.append(total)
    grad = jnp.concatenate(halves, axis=0) / replicas
    state = state_ref[...] + jnp.mean(grad * grad, axis=1, keepdims=True)
    out_ref[0:mine, :] = (
        previous_ref[...].astype(f32) - learn_rate * grad / (jnp.sqrt(state) + epsilon)
    ).astype(bf16)
    at = iota((chunk, width), 1) == iota((chunk, width), 0) + offset_ref[0]
    sub = iota((16, width), 0)
    lines = jnp.zeros((16, width), f32)
    for core in range(2):
        own = state[core * chunk : (core + 1) * chunk]
        line = jnp.sum(jnp.where(at, own, 0.0), axis=0, keepdims=True)
        first = line.astype(bf16).astype(f32)
        second = (line - first).astype(bf16).astype(f32)
        for k, piece in enumerate((first, second, line - first - second)):
            lines = jnp.where(sub == 3 * core + k, piece, lines)
    out_ref[mine : mine + 16, :] = lines.astype(bf16)


def update_rows(offset, parts, previous, state):
    _, chunk, width = parts.shape
    mine = 2 * chunk
    vmem = pl.BlockSpec(memory_space=pltpu.VMEM)
    return pl.pallas_call(
        update_kernel,
        out_shape=jax.ShapeDtypeStruct((mine + 16, width), bf16),
        in_specs=[pl.BlockSpec(memory_space=pltpu.SMEM), vmem, vmem, vmem],
        compiler_params=params,
        name="update",
    )(offset, parts, previous, state)


def place_kernel(
    mine, starts, every_ref, listed_ref, tiles_ref, table_ref, state_ref, out_ref, state_out, values
):
    step = pl.program_id(0)
    rows, width = table_ref.shape
    touch = listed_ref.shape[1]
    replicas = touch // mine
    stride = mine + 16

    @pl.when(step == 0)
    def _():
        values[touch:, :] = jnp.zeros((256, width), bf16)
        chunk = mine // 2
        for k in range(replicas):
            for core in range(2):
                at = core * (touch // 2) + k * chunk
                source = k * stride + core * chunk
                values[at : at + chunk, :] = every_ref[source : source + chunk, :]
        group = width // chunk
        pieces = []
        for q in range(replicas // group):
            lines = jnp.zeros((16, width), f32)
            for k in range(q * group, (q + 1) * group):
                lines = lines + every_ref[k * stride + mine : (k + 1) * stride, :].astype(f32)
            pieces.append(lines)
        lines = jnp.concatenate(
            [lines[3 * core : 3 * core + 3] for core in range(2) for lines in pieces], axis=1
        )
        high = state_ref.shape[0]
        listed = listed_ref[...]
        at_high = iota((high, touch), 0) == (listed >> 7)
        spread = jnp.concatenate(
            [jnp.where(at_high, lines[k : k + 1, :], 0.0) for k in range(3)], axis=0
        ).astype(bf16)
        at_low = jnp.where(iota((128, touch), 0) == (listed & 127), 1.0, 0.0).astype(bf16)
        placed = dot_nt(spread, at_low)
        state_out[...] = state_ref[...] + (
            placed[0:high] + placed[high : 2 * high] + placed[2 * high : 3 * high]
        )

    for k in range(rows // 128):
        at = step * (rows // 128) + k
        tile = starts[at] >> 7
        row = iota((128, 128), 0) + at * 128
        chosen = jnp.concatenate(
            [
                jnp.where(row == tiles_ref[pl.ds(tile + n, 1), :], 1.0, 0.0).astype(bf16)
                for n in range(2)
            ],
            axis=1,
        )
        window = values[pl.ds(pl.multiple_of(tile * 128, 128), 256), :]
        here = slice(k * 128, (k + 1) * 128)
        out_ref[here, :] = (table_ref[here, :].astype(f32) + dot(chosen, window)).astype(bf16)


def place_rows(starts, every, listed, table, state, mine, tile):
    rows, width = table.shape
    touch = listed.shape[1]
    high = rows // 128
    tiles = jnp.pad(listed.reshape(touch // 128, 128), ((0, 8), (0, 0)), constant_values=-1)
    whole = lambda i, starts: (0, 0)
    return pl.pallas_call(
        functools.partial(place_kernel, mine),
        grid_spec=pltpu.PrefetchScalarGridSpec(
            num_scalar_prefetch=1,
            grid=(rows // tile,),
            in_specs=[
                pl.BlockSpec(every.shape, whole),
                pl.BlockSpec(listed.shape, whole),
                pl.BlockSpec(tiles.shape, whole),
                pl.BlockSpec((tile, width), lambda i, starts: (i, 0)),
                pl.BlockSpec((high, 128), whole),
            ],
            out_specs=(
                pl.BlockSpec((tile, width), lambda i, starts: (i, 0)),
                pl.BlockSpec((high, 128), whole),
            ),
            scratch_shapes=[pltpu.VMEM((touch + 256, width), bf16)],
        ),
        out_shape=(
            jax.ShapeDtypeStruct((rows, width), bf16),
            jax.ShapeDtypeStruct((high, 128), f32),
        ),
        compiler_params=params,
        name="place",
    )(starts, every, listed, tiles, table, state.reshape(high, 128))


def pool_kernel(member_ref, rows_ref, out_ref):
    bag_count = out_ref.shape[0]
    total = dot(member_ref[...], rows_ref[...])
    out_ref[...] = jnp.concatenate([total[0:bag_count], total[64 : 64 + bag_count]], axis=1)


def pool_rows(member, rows, bag_count):
    return pl.pallas_call(
        pool_kernel,
        out_shape=jax.ShapeDtypeStruct((bag_count, 2 * rows.shape[1]), f32),
        compiler_params=params,
        name="pool",
    )(member, rows)


def local(table, row_state, touched_rows, lookup_rows, lookup_bags, route_counts, pooled_grad):
    shards = lax.axis_size("shard")
    replicas = lax.axis_size("replica")
    capacity = lookup_rows.shape[2]
    bag_count, width = pooled_grad.shape
    touch = touched_rows.shape[0]
    mine = touch // replicas
    rows = row_state.shape[0]
    tile = 1024

    bags = jnp.transpose(lookup_bags, (2, 0, 1))
    send = prep(jnp.transpose(lookup_rows, (2, 0, 1)), bags, route_counts, pooled_grad)
    got = lax.all_to_all(
        send.reshape(shards, block, width), "shard", split_axis=0, concat_axis=0, tiled=True
    ).reshape(shards * block, width)

    listed = sort_list(touched_rows)
    replica = lax.axis_index("replica")
    half = touch // 2
    order = listed.reshape(touch)
    core = lax.rem(replica, 2)
    theirs = lax.dynamic_slice(order, ((1 - core) * half,), (half,))
    ours = lax.dynamic_slice(order, (core * half,), (half,))
    turned = jnp.concatenate([theirs, ours])
    column = jnp.broadcast_to(turned.reshape(touch, 1).astype(f32), (touch, 128))
    bounds = jnp.arange(rows // 128, dtype=jnp.int32) * 128
    starts = jnp.sum((touched_rows[None, :] < bounds[:, None]).astype(jnp.int32), axis=1)
    values = jnp.take(table, turned, axis=0, mode="clip")
    chunk = mine // 2
    mine_rows = lax.dynamic_slice(order.reshape(2, half), (0, replica * chunk), (2, chunk))
    mine_rows = mine_rows.reshape(mine)
    mine_values = jnp.take(table, mine_rows, axis=0, mode="clip")
    mine_state = jnp.take(row_state, mine_rows, mode="clip")[:, None]
    marked = jnp.zeros(row_state.shape, f32).at[touched_rows].set(
        1.0, mode="promise_in_bounds", unique_indices=True
    )
    kept_state = jnp.where(marked > 0, 0.0, row_state)
    kept_table = jnp.where(marked[:, None] > 0, jnp.zeros((), bf16), table)
    got, column, values, kept_state, kept_table, mine_state, mine_values, starts = (
        lax.optimization_barrier(
            (got, column, values, kept_state, kept_table, mine_state, mine_values, starts)
        )
    )

    theirs, ours = partial_sums(got, column, capacity)
    pairs = [[k, k + 1] for k in range(0, replicas, 2)]
    both = lax.all_gather(theirs, "replica", axis=0, tiled=True, axis_index_groups=pairs)
    theirs = lax.dynamic_slice(both, ((1 - core) * half, 0), (half, width))
    part = (ours + theirs.astype(f32)).astype(bf16)
    parts = lax.all_to_all(
        part.reshape(replicas, chunk, width), "replica", split_axis=0, concat_axis=0, tiled=True
    )
    picked = pick_rows(got, column, values, shards, capacity)
    member = member_matrix(bags, route_counts)
    offset = (lax.rem(replica, width // chunk) * chunk).astype(jnp.int32).reshape(1)
    picked, member, parts = lax.optimization_barrier((picked, member, parts))
    returned = lax.all_to_all(picked, "shard", split_axis=0, concat_axis=0, tiled=True)
    updated = update_rows(offset, parts, mine_values, mine_state)
    every = lax.all_gather(updated, "replica", axis=0, tiled=True)
    new_table, new_state = place_rows(starts, every, listed, kept_table, kept_state, mine, tile)
    pooled = pool_rows(member, returned.reshape(-1, width // 2), bag_count)
    return (pooled, new_table, new_state.reshape(row_state.shape))


def solution(mesh):
    return jax.shard_map(
        local,
        mesh=mesh,
        in_specs=(
            P("shard", None),
            P("shard"),
            P("shard"),
            P("replica", "shard", None),
            P("replica", "shard", None),
            P("replica", "shard"),
            P(("replica", "shard"), None),
        ),
        out_specs=(P(("replica", "shard"), None), P("shard", None), P("shard")),
        check_vma=False,
    )
```

```python
import functools

import jax
import jax.numpy as jnp
from jax import lax
from jax.experimental import pallas as pl
from jax.experimental.pallas import tpu as pltpu
from jax.sharding import PartitionSpec as P

learn_rate = 0.5
epsilon = 1e-08
bf16 = jnp.bfloat16
f32 = jnp.float32

block = 24
dead = 200
large = pltpu.CompilerParams(vmem_limit_bytes=60 * 1024 * 1024)
params = pltpu.CompilerParams(vmem_limit_bytes=24 * 1024 * 1024)


def iota(shape, axis):
    return lax.broadcasted_iota(jnp.int32, shape, axis)


def dot(a, b):
    return jnp.dot(a, b, preferred_element_type=f32)


def pair_of(position):
    return (position * 2731) >> 16


def keys_of(bags_ref, counts_ref):
    capacity, _, shards = bags_ref.shape
    bags = bags_ref[...].reshape(capacity, shards)
    live = iota((capacity, shards), 0) < counts_ref[...]
    return jnp.where(live, bags, dead).astype(f32).astype(bf16)


def dot_nt(a, b):
    return lax.dot_general(a, b, (((1,), (1,)), ((), ())), preferred_element_type=f32)


def dot_tn(a, b):
    return lax.dot_general(a, b, (((0,), (0,)), ((), ())), preferred_element_type=f32)


def prep_kernel(rows_ref, bags_ref, counts_ref, grad_ref, out_ref, held, sems):
    capacity, _, shards = rows_ref.shape
    bag_count, width = grad_ref.shape
    flat = shards * block
    key = keys_of(bags_ref, counts_ref)
    position, lane = iota((flat, 128), 0), iota((flat, 128), 1)
    pair = pair_of(position)
    slot = position - block * pair
    spread = jnp.where(pair == lane, 1.0, 0.0)
    per_row = dot_nt(spread.astype(bf16)[:, 0:shards], key)
    per_row = jnp.where((slot == lane)[:, 0:capacity], per_row, 0.0).astype(bf16)
    bag = dot(per_row, jnp.ones((capacity, 128), bf16))
    bag = jnp.where(slot < capacity, bag, float(dead))
    member = jnp.where(bag == lane.astype(f32), 1.0, 0.0).astype(bf16)
    grads = jnp.concatenate(
        [grad_ref[...], jnp.zeros((128 - bag_count, width), f32)], axis=0
    ).astype(bf16)
    rows = rows_ref[...].reshape(capacity, shards)
    high = (rows >> 6).astype(f32).astype(bf16)
    low = (rows & 63).astype(f32).astype(bf16)
    lane = iota((width, capacity), 0)
    sub = iota((width, capacity), 1)
    meta = dot(jnp.where(lane == sub, 1.0, 0.0).astype(bf16), high) + dot(
        jnp.where(lane == sub + 128, 1.0, 0.0).astype(bf16), low
    )
    at_meta = jnp.where(slot == capacity, spread, 0.0).astype(bf16)[:, 0:shards]
    meta = meta.astype(bf16)
    pieces = sems.shape[0]
    size = flat // pieces
    copies = []
    for k in range(pieces):
        here = slice(k * size, (k + 1) * size)
        held[here, :] = (dot(member[here], grads) + dot_nt(at_meta[here], meta)).astype(bf16)
        at = pl.ds(k * size, size)
        copies.append(pltpu.make_async_copy(held.at[at], out_ref.at[at], sems.at[k]))
        copies[-1].start()
    for copy in copies:
        copy.wait()


def prep(rows, bags, counts, grad):
    shards = rows.shape[2]
    return pl.pallas_call(
        prep_kernel,
        out_shape=jax.ShapeDtypeStruct((shards * block, grad.shape[1]), bf16),
        out_specs=pl.BlockSpec(memory_space=pltpu.HBM),
        scratch_shapes=[
            pltpu.VMEM((shards * block, grad.shape[1]), bf16),
            pltpu.SemaphoreType.DMA((4,)),
        ],
        compiler_params=large,
        name="prep",
    )(rows, bags, counts, grad)


def packed_slot(position, capacity):
    whole = 16
    rest = capacity - whole
    tail = position - 2 * whole
    right = ((position >= whole) & (position < 2 * whole)) | (tail >= rest)
    slot = jnp.where(
        position < 2 * whole,
        position & (whole - 1),
        whole + jnp.where(tail >= rest, tail - rest, tail),
    )
    return slot, right


def member_kernel(bags_ref, counts_ref, out_ref):
    capacity, _, shards = bags_ref.shape
    pack = 2 * capacity
    flat = shards * pack
    key = keys_of(bags_ref, counts_ref)

    def pair_and_place(shape, axis):
        row = iota(shape, axis)
        pair = (row * 13108) >> 19
        return pair, row - pack * pair

    shape = (shards, flat)
    spread = jnp.where(pair_and_place(shape, 1)[0] == iota(shape, 0), 1.0, 0.0).astype(bf16)
    per_row = dot(key, spread)
    shape = (capacity, flat)
    slot, _ = packed_slot(pair_and_place(shape, 1)[1], capacity)
    own = jnp.where(slot == iota(shape, 0), per_row, 0.0).astype(bf16)
    bag = dot(jnp.ones((128, capacity), bf16), own)
    shape = (128, flat)
    _, right = packed_slot(pair_and_place(shape, 1)[1], capacity)
    bag = bag + jnp.where(right, 64.0, 0.0)
    out_ref[...] = jnp.where(bag == iota(shape, 0).astype(f32), 1.0, 0.0).astype(bf16)


def member_matrix(bags, counts):
    capacity, _, shards = bags.shape
    return pl.pallas_call(
        member_kernel,
        out_shape=jax.ShapeDtypeStruct((128, shards * 2 * capacity), bf16),
        compiler_params=params,
        name="member",
    )(bags, counts)


def sort_kernel(line_ref, column_ref, line_out):
    touch = line_ref.shape[1]
    tiles = touch // 128
    column = jnp.broadcast_to(column_ref[...], (touch, 128))
    lanes = iota((touch, 128), 1).astype(f32)
    below = jnp.zeros((touch, 128), f32)
    for k in range(tiles):
        line = line_ref[:, k * 128 : (k + 1) * 128]
        below = below + jnp.where(line < column, 1.0, 0.0)
    rank_column = jnp.sum(below, axis=1, keepdims=True)
    for k in range(tiles):
        at = rank_column == lanes + 128.0 * k
        line_out[:, k * 128 : (k + 1) * 128] = jnp.sum(
            jnp.where(at, column, 0.0), axis=0, keepdims=True
        ).astype(jnp.int32)


def sort_list(touched):
    touch = touched.shape[0]
    values = touched.astype(f32)
    return pl.pallas_call(
        sort_kernel,
        out_shape=jax.ShapeDtypeStruct((1, touch), jnp.int32),
        compiler_params=params,
        name="sort",
    )(values.reshape(1, touch), values.reshape(touch, 1))


def hit_matrix(got_ref, column_ref, hits, capacity):
    flat, width = got_ref.shape
    shards = flat // block
    column = column_ref[...]
    got = got_ref[...]
    meta = got.astype(f32).reshape(shards, block, width)[:, capacity : capacity + 1, :]
    shape = (shards, block, width)
    own = (iota(shape, 2) & 127) == iota(shape, 1)
    spread = jnp.where(own, jnp.broadcast_to(meta, shape), 0.0).reshape(flat, width).astype(bf16)
    weigh = jnp.where(iota((8, width), 1) < 128, 64.0, 1.0).astype(bf16)
    rows = dot_nt(weigh, spread)
    lane = iota((8, flat), 1)
    rows = jnp.where(lane - block * pair_of(lane) < capacity, rows, -1.0)
    for k in range(flat // 128):
        line = rows[0:1, k * 128 : (k + 1) * 128]
        hits[:, k * 128 : (k + 1) * 128] = jnp.where(column == line, 1.0, 0.0).astype(bf16)
    return got


def hits_kernel(
    capacity, got_ref, column_ref, values_ref, theirs_ref, ours_ref, picked_ref, hits
):
    got = hit_matrix(got_ref, column_ref, hits, capacity)
    half = theirs_ref.shape[0]
    theirs_ref[...] = dot(hits[0:half, :], got).astype(bf16)
    ours_ref[...] = dot(hits[half:, :], got)
    shards, pack, width = picked_ref.shape
    whole = 16
    rest = pack // 2 - whole
    rows = dot_tn(hits[...], values_ref[...]).reshape(shards, block, 2 * width)
    left, right = rows[:, :, 0:width], rows[:, :, width : 2 * width]
    first = iota((shards, block - whole, width), 1) < rest
    mixed = jnp.where(
        first, left[:, whole:block, :], pltpu.roll(right[:, whole:block, :], rest, 1)
    )
    picked_ref[...] = jnp.concatenate(
        [left[:, 0:whole, :], right[:, 0:whole, :], mixed], axis=1
    ).astype(bf16)


def sums_and_rows(got, column, values, shards, capacity):
    flat, width = got.shape
    touch = column.shape[0]
    return pl.pallas_call(
        functools.partial(hits_kernel, capacity),
        out_shape=(
            jax.ShapeDtypeStruct((touch // 2, width), bf16),
            jax.ShapeDtypeStruct((touch // 2, width), f32),
            jax.ShapeDtypeStruct((shards, 2 * capacity, width // 2), bf16),
        ),
        scratch_shapes=[pltpu.VMEM((touch, flat), bf16)],
        compiler_params=params,
        name="hits",
    )(got, column, values)


def update_kernel(offset_ref, parts_ref, previous_ref, state_ref, out_ref):
    replicas, chunk, width = parts_ref.shape
    mine = 2 * chunk
    halves = []
    for core in range(2):
        total = parts_ref[core].astype(f32)
        for k in range(core + 2, replicas, 2):
            total = total + parts_ref[k].astype(f32)
        halves.append(total)
    grad = jnp.concatenate(halves, axis=0) / replicas
    state = state_ref[...] + jnp.mean(grad * grad, axis=1, keepdims=True)
    out_ref[0:mine, :] = (
        previous_ref[...].astype(f32) - learn_rate * grad / (jnp.sqrt(state) + epsilon)
    ).astype(bf16)
    at = iota((chunk, width), 1) == iota((chunk, width), 0) + offset_ref[0]
    sub = iota((16, width), 0)
    lines = jnp.zeros((16, width), f32)
    for core in range(2):
        own = state[core * chunk : (core + 1) * chunk]
        line = jnp.sum(jnp.where(at, own, 0.0), axis=0, keepdims=True)
        first = line.astype(bf16).astype(f32)
        second = (line - first).astype(bf16).astype(f32)
        for k, piece in enumerate((first, second, line - first - second)):
            lines = jnp.where(sub == 3 * core + k, piece, lines)
    out_ref[mine : mine + 16, :] = lines.astype(bf16)


def update_rows(offset, parts, previous, state):
    _, chunk, width = parts.shape
    mine = 2 * chunk
    vmem = pl.BlockSpec(memory_space=pltpu.VMEM)
    return pl.pallas_call(
        update_kernel,
        out_shape=jax.ShapeDtypeStruct((mine + 16, width), bf16),
        in_specs=[pl.BlockSpec(memory_space=pltpu.SMEM), vmem, vmem, vmem],
        compiler_params=params,
        name="update",
    )(offset, parts, previous, state)


def place_kernel(
    mine, starts, every_ref, listed_ref, tiles_ref, table_ref, state_ref, out_ref, state_out, values
):
    step = pl.program_id(0)
    rows, width = table_ref.shape
    touch = listed_ref.shape[1]
    replicas = touch // mine
    stride = mine + 16

    @pl.when(step == 0)
    def _():
        values[touch:, :] = jnp.zeros((256, width), bf16)
        chunk = mine // 2
        for k in range(replicas):
            for core in range(2):
                at = core * (touch // 2) + k * chunk
                source = k * stride + core * chunk
                values[at : at + chunk, :] = every_ref[source : source + chunk, :]
        group = width // chunk
        pieces = []
        for q in range(replicas // group):
            lines = jnp.zeros((16, width), f32)
            for k in range(q * group, (q + 1) * group):
                lines = lines + every_ref[k * stride + mine : (k + 1) * stride, :].astype(f32)
            pieces.append(lines)
        lines = jnp.concatenate(
            [lines[3 * core : 3 * core + 3] for core in range(2) for lines in pieces], axis=1
        )
        high = state_ref.shape[0]
        listed = listed_ref[...]
        at_high = iota((high, touch), 0) == (listed >> 7)
        spread = jnp.concatenate(
            [jnp.where(at_high, lines[k : k + 1, :], 0.0) for k in range(3)], axis=0
        ).astype(bf16)
        at_low = jnp.where(iota((128, touch), 0) == (listed & 127), 1.0, 0.0).astype(bf16)
        placed = dot_nt(spread, at_low)
        state_out[...] = state_ref[...] + (
            placed[0:high] + placed[high : 2 * high] + placed[2 * high : 3 * high]
        )

    for k in range(rows // 128):
        at = step * (rows // 128) + k
        tile = starts[at] >> 7
        row = iota((128, 128), 0) + at * 128
        chosen = jnp.concatenate(
            [
                jnp.where(row == tiles_ref[pl.ds(tile + n, 1), :], 1.0, 0.0).astype(bf16)
                for n in range(2)
            ],
            axis=1,
        )
        window = values[pl.ds(pl.multiple_of(tile * 128, 128), 256), :]
        here = slice(k * 128, (k + 1) * 128)
        out_ref[here, :] = (table_ref[here, :].astype(f32) + dot(chosen, window)).astype(bf16)


def place_rows(starts, every, listed, table, state, mine, tile):
    rows, width = table.shape
    touch = listed.shape[1]
    high = rows // 128
    tiles = jnp.pad(listed.reshape(touch // 128, 128), ((0, 8), (0, 0)), constant_values=-1)
    whole = lambda i, starts: (0, 0)
    return pl.pallas_call(
        functools.partial(place_kernel, mine),
        grid_spec=pltpu.PrefetchScalarGridSpec(
            num_scalar_prefetch=1,
            grid=(rows // tile,),
            in_specs=[
                pl.BlockSpec(every.shape, whole),
                pl.BlockSpec(listed.shape, whole),
                pl.BlockSpec(tiles.shape, whole),
                pl.BlockSpec((tile, width), lambda i, starts: (i, 0)),
                pl.BlockSpec((high, 128), whole),
            ],
            out_specs=(
                pl.BlockSpec((tile, width), lambda i, starts: (i, 0)),
                pl.BlockSpec((high, 128), whole),
            ),
            scratch_shapes=[pltpu.VMEM((touch + 256, width), bf16)],
        ),
        out_shape=(
            jax.ShapeDtypeStruct((rows, width), bf16),
            jax.ShapeDtypeStruct((high, 128), f32),
        ),
        compiler_params=params,
        name="place",
    )(starts, every, listed, tiles, table, state.reshape(high, 128))


def pool_kernel(member_ref, rows_ref, out_ref):
    bag_count = out_ref.shape[0]
    total = dot(member_ref[...], rows_ref[...])
    out_ref[...] = jnp.concatenate([total[0:bag_count], total[64 : 64 + bag_count]], axis=1)


def pool_rows(member, rows, bag_count):
    return pl.pallas_call(
        pool_kernel,
        out_shape=jax.ShapeDtypeStruct((bag_count, 2 * rows.shape[1]), f32),
        compiler_params=params,
        name="pool",
    )(member, rows)


def local(table, row_state, touched_rows, lookup_rows, lookup_bags, route_counts, pooled_grad):
    shards = lax.axis_size("shard")
    replicas = lax.axis_size("replica")
    capacity = lookup_rows.shape[2]
    bag_count, width = pooled_grad.shape
    touch = touched_rows.shape[0]
    mine = touch // replicas
    rows = row_state.shape[0]
    tile = 1024

    bags = jnp.transpose(lookup_bags, (2, 0, 1))
    send = prep(jnp.transpose(lookup_rows, (2, 0, 1)), bags, route_counts, pooled_grad)
    got = lax.all_to_all(
        send.reshape(shards, block, width), "shard", split_axis=0, concat_axis=0, tiled=True
    ).reshape(shards * block, width)

    listed = sort_list(touched_rows)
    replica = lax.axis_index("replica")
    half = touch // 2
    order = listed.reshape(touch)
    core = lax.rem(replica, 2)
    theirs = lax.dynamic_slice(order, ((1 - core) * half,), (half,))
    ours = lax.dynamic_slice(order, (core * half,), (half,))
    turned = jnp.concatenate([theirs, ours])
    column = jnp.broadcast_to(turned.reshape(touch, 1).astype(f32), (touch, 128))
    bounds = jnp.arange(rows // 128, dtype=jnp.int32) * 128
    starts = jnp.sum((touched_rows[None, :] < bounds[:, None]).astype(jnp.int32), axis=1)
    values = jnp.take(table, turned, axis=0, mode="clip")
    chunk = mine // 2
    mine_rows = lax.dynamic_slice(order.reshape(2, half), (0, replica * chunk), (2, chunk))
    mine_rows = mine_rows.reshape(mine)
    mine_values = jnp.concatenate(
        [
            lax.dynamic_slice(values, ((1 - core) * half + replica * chunk, 0), (chunk, width)),
            lax.dynamic_slice(values, (core * half + replica * chunk, 0), (chunk, width)),
        ]
    )
    mine_state = jnp.take(row_state, mine_rows, mode="clip")[:, None]
    marked = jnp.zeros(row_state.shape, f32).at[touched_rows].set(
        1.0, mode="promise_in_bounds", unique_indices=True
    )
    kept_state = jnp.where(marked > 0, 0.0, row_state)
    kept_table = jnp.where(marked[:, None] > 0, jnp.zeros((), bf16), table)
    member = member_matrix(bags, route_counts)
    got, column, values, kept_state, kept_table, mine_state, mine_values, starts, member = (
        lax.optimization_barrier(
            (got, column, values, kept_state, kept_table, mine_state, mine_values, starts, member)
        )
    )

    theirs, ours, picked = sums_and_rows(got, column, values, shards, capacity)
    pairs = [[k, k + 1] for k in range(0, replicas, 2)]
    both = lax.all_gather(theirs, "replica", axis=0, tiled=True, axis_index_groups=pairs)
    theirs = lax.dynamic_slice(both, ((1 - core) * half, 0), (half, width))
    part = (ours + theirs.astype(f32)).astype(bf16)
    parts = lax.all_to_all(
        part.reshape(replicas, chunk, width), "replica", split_axis=0, concat_axis=0, tiled=True
    )
    offset = (lax.rem(replica, width // chunk) * chunk).astype(jnp.int32).reshape(1)
    picked, parts = lax.optimization_barrier((picked, parts))
    returned = lax.all_to_all(picked, "shard", split_axis=0, concat_axis=0, tiled=True)
    updated = update_rows(offset, parts, mine_values, mine_state)
    every = lax.all_gather(updated, "replica", axis=0, tiled=True)
    new_table, new_state = place_rows(starts, every, listed, kept_table, kept_state, mine, tile)
    pooled = pool_rows(member, returned.reshape(-1, width // 2), bag_count)
    return (pooled, new_table, new_state.reshape(row_state.shape))


def solution(mesh):
    return jax.shard_map(
        local,
        mesh=mesh,
        in_specs=(
            P("shard", None),
            P("shard"),
            P("shard"),
            P("replica", "shard", None),
            P("replica", "shard", None),
            P("replica", "shard"),
            P(("replica", "shard"), None),
        ),
        out_specs=(P(("replica", "shard"), None), P("shard", None), P("shard")),
        check_vma=False,
    )
```

```python
import functools

import jax
import jax.numpy as jnp
from jax import lax
from jax.experimental import pallas as pl
from jax.experimental.pallas import tpu as pltpu
from jax.sharding import PartitionSpec as P

learn_rate = 0.5
epsilon = 1e-08
bf16 = jnp.bfloat16
f32 = jnp.float32

block = 24
dead = 200
large = pltpu.CompilerParams(vmem_limit_bytes=60 * 1024 * 1024)
params = pltpu.CompilerParams(vmem_limit_bytes=24 * 1024 * 1024)


def iota(shape, axis):
    return lax.broadcasted_iota(jnp.int32, shape, axis)


def dot(a, b):
    return jnp.dot(a, b, preferred_element_type=f32)


def pair_of(position):
    return (position * 2731) >> 16


def keys_of(bags_ref, counts_ref):
    capacity, _, shards = bags_ref.shape
    bags = bags_ref[...].reshape(capacity, shards)
    live = iota((capacity, shards), 0) < counts_ref[...]
    return jnp.where(live, bags, dead).astype(f32).astype(bf16)


def dot_nt(a, b):
    return lax.dot_general(a, b, (((1,), (1,)), ((), ())), preferred_element_type=f32)


def dot_tn(a, b):
    return lax.dot_general(a, b, (((0,), (0,)), ((), ())), preferred_element_type=f32)


def prep_kernel(rows_ref, bags_ref, counts_ref, grad_ref, out_ref, held, sems):
    capacity, _, shards = rows_ref.shape
    bag_count, width = grad_ref.shape
    flat = shards * block
    groups = held.shape[1]
    key = keys_of(bags_ref, counts_ref)
    position, lane = iota((flat, 128), 0), iota((flat, 128), 1)
    pair = pair_of(position)
    slot = position - block * pair
    spread = jnp.where(pair == lane, 1.0, 0.0)
    per_row = dot_nt(spread.astype(bf16)[:, 0:shards], key)
    per_row = jnp.where((slot == lane)[:, 0:capacity], per_row, 0.0).astype(bf16)
    bag = dot(per_row, jnp.ones((capacity, 128), bf16))
    bag = jnp.where(slot < capacity, bag, float(dead))
    member = jnp.where(bag == lane.astype(f32), 1.0, 0.0).astype(bf16)
    grads = jnp.concatenate(
        [grad_ref[...], jnp.zeros((128 - bag_count, width), f32)], axis=0
    ).astype(bf16)
    rows = rows_ref[...].reshape(capacity, shards)
    high = (rows >> 6).astype(f32).astype(bf16)
    low = (rows & 63).astype(f32).astype(bf16)
    lane = iota((width, capacity), 0)
    sub = iota((width, capacity), 1)
    meta = dot(jnp.where(lane == sub, 1.0, 0.0).astype(bf16), high) + dot(
        jnp.where(lane == sub + 64, 1.0, 0.0).astype(bf16), low
    )
    at_meta = jnp.where(slot == capacity, spread, 0.0).astype(bf16)[:, 0:shards]
    meta = meta.astype(bf16)
    pieces = sems.shape[0]
    size = flat // pieces
    copies = []
    for k in range(pieces):
        here = slice(k * size, (k + 1) * size)
        rows = dot(member[here], grads) + dot_nt(at_meta[here], meta)
        pairs = shards // pieces
        rows = rows.reshape(pairs, block, width)
        to = slice(k * pairs, (k + 1) * pairs)
        for g in range(groups - 1):
            q, h = g // 2, (g % 2) * 128
            held[to, g] = rows[:, 4 * q : 4 * q + 4, h : h + 128].astype(bf16)
        held[to, groups - 1] = rows[:, capacity : capacity + 4, 0:128].astype(bf16)
        at = pl.ds(k * pairs, pairs)
        copies.append(pltpu.make_async_copy(held.at[at], out_ref.at[at], sems.at[k]))
        copies[-1].start()
    for copy in copies:
        copy.wait()


def prep(rows, bags, counts, grad):
    capacity, _, shards = rows.shape
    shape = (shards, capacity // 2 + 1, 4, 128)
    return pl.pallas_call(
        prep_kernel,
        out_shape=jax.ShapeDtypeStruct(shape, bf16),
        out_specs=pl.BlockSpec(memory_space=pltpu.HBM),
        scratch_shapes=[pltpu.VMEM(shape, bf16), pltpu.SemaphoreType.DMA((4,))],
        compiler_params=large,
        name="prep",
    )(rows, bags, counts, grad)


def packed_slot(position, capacity):
    whole = 16
    rest = capacity - whole
    tail = position - 2 * whole
    right = ((position >= whole) & (position < 2 * whole)) | (tail >= rest)
    slot = jnp.where(
        position < 2 * whole,
        position & (whole - 1),
        whole + jnp.where(tail >= rest, tail - rest, tail),
    )
    return slot, right


def member_kernel(bags_ref, counts_ref, out_ref):
    capacity, _, shards = bags_ref.shape
    pack = 2 * capacity
    flat = shards * pack
    key = keys_of(bags_ref, counts_ref)

    def pair_and_place(shape, axis):
        row = iota(shape, axis)
        pair = (row * 13108) >> 19
        return pair, row - pack * pair

    shape = (shards, flat)
    spread = jnp.where(pair_and_place(shape, 1)[0] == iota(shape, 0), 1.0, 0.0).astype(bf16)
    per_row = dot(key, spread)
    shape = (capacity, flat)
    slot, _ = packed_slot(pair_and_place(shape, 1)[1], capacity)
    own = jnp.where(slot == iota(shape, 0), per_row, 0.0).astype(bf16)
    bag = dot(jnp.ones((128, capacity), bf16), own)
    shape = (128, flat)
    _, right = packed_slot(pair_and_place(shape, 1)[1], capacity)
    bag = bag + jnp.where(right, 64.0, 0.0)
    out_ref[...] = jnp.where(bag == iota(shape, 0).astype(f32), 1.0, 0.0).astype(bf16)


def member_matrix(bags, counts):
    capacity, _, shards = bags.shape
    return pl.pallas_call(
        member_kernel,
        out_shape=jax.ShapeDtypeStruct((128, shards * 2 * capacity), bf16),
        compiler_params=params,
        name="member",
    )(bags, counts)


def sort_kernel(line_ref, column_ref, line_out):
    touch = line_ref.shape[1]
    tiles = touch // 128
    column = jnp.broadcast_to(column_ref[...], (touch, 128))
    lanes = iota((touch, 128), 1).astype(f32)
    below = jnp.zeros((touch, 128), f32)
    for k in range(tiles):
        line = line_ref[:, k * 128 : (k + 1) * 128]
        below = below + jnp.where(line < column, 1.0, 0.0)
    rank_column = jnp.sum(below, axis=1, keepdims=True)
    for k in range(tiles):
        at = rank_column == lanes + 128.0 * k
        line_out[:, k * 128 : (k + 1) * 128] = jnp.sum(
            jnp.where(at, column, 0.0), axis=0, keepdims=True
        ).astype(jnp.int32)


def sort_list(touched):
    touch = touched.shape[0]
    values = touched.astype(f32)
    return pl.pallas_call(
        sort_kernel,
        out_shape=jax.ShapeDtypeStruct((1, touch), jnp.int32),
        compiler_params=params,
        name="sort",
    )(values.reshape(1, touch), values.reshape(touch, 1))


def hit_matrix(got_ref, column_ref, hits, capacity):
    shards, groups, _, half = got_ref.shape
    flat = shards * block
    left = [got_ref[:, g].astype(f32) for g in range(0, groups - 1, 2)]
    right = [got_ref[:, g].astype(f32) for g in range(1, groups - 1, 2)]
    meta = got_ref[:, groups - 1].astype(f32)
    none = jnp.zeros(meta.shape, f32)
    got = jnp.concatenate(
        [jnp.concatenate(left + [none], axis=1), jnp.concatenate(right + [none], axis=1)], axis=2
    )
    got = got.reshape(flat, 2 * half).astype(bf16)
    column = column_ref[...]
    shape = (shards, block, half)
    own = (iota(shape, 2) & 63) == iota(shape, 1)
    spread = jnp.where(own, jnp.broadcast_to(meta[:, 0:1, :], shape), 0.0)
    spread = spread.reshape(flat, half).astype(bf16)
    weigh = jnp.where(iota((8, half), 1) < 64, 64.0, 1.0).astype(bf16)
    rows = dot_nt(weigh, spread)
    lane = iota((8, flat), 1)
    rows = jnp.where(lane - block * pair_of(lane) < capacity, rows, -1.0)
    for k in range(flat // 128):
        line = rows[0:1, k * 128 : (k + 1) * 128]
        hits[:, k * 128 : (k + 1) * 128] = jnp.where(column == line, 1.0, 0.0).astype(bf16)
    return got


def hits_kernel(
    capacity, got_ref, column_ref, values_ref, theirs_ref, ours_ref, picked_ref, hits
):
    got = hit_matrix(got_ref, column_ref, hits, capacity)
    half = theirs_ref.shape[0]
    theirs_ref[...] = dot(hits[0:half, :], got).astype(bf16)
    ours_ref[...] = dot(hits[half:, :], got)
    shards, pack, width = picked_ref.shape
    whole = 16
    rest = pack // 2 - whole
    rows = dot_tn(hits[...], values_ref[...]).reshape(shards, block, 2 * width)
    left, right = rows[:, :, 0:width], rows[:, :, width : 2 * width]
    first = iota((shards, block - whole, width), 1) < rest
    mixed = jnp.where(
        first, left[:, whole:block, :], pltpu.roll(right[:, whole:block, :], rest, 1)
    )
    picked_ref[...] = jnp.concatenate(
        [left[:, 0:whole, :], right[:, 0:whole, :], mixed], axis=1
    ).astype(bf16)


def sums_and_rows(got, column, values, shards, capacity):
    flat, width = shards * block, values.shape[1]
    touch = column.shape[0]
    return pl.pallas_call(
        functools.partial(hits_kernel, capacity),
        out_shape=(
            jax.ShapeDtypeStruct((touch // 2, width), bf16),
            jax.ShapeDtypeStruct((touch // 2, width), f32),
            jax.ShapeDtypeStruct((shards, 2 * capacity, width // 2), bf16),
        ),
        scratch_shapes=[pltpu.VMEM((touch, flat), bf16)],
        compiler_params=params,
        name="hits",
    )(got, column, values)


def update_kernel(offset_ref, parts_ref, previous_ref, state_ref, out_ref):
    replicas, chunk, width = parts_ref.shape
    mine = 2 * chunk
    halves = []
    for core in range(2):
        total = parts_ref[core].astype(f32)
        for k in range(core + 2, replicas, 2):
            total = total + parts_ref[k].astype(f32)
        halves.append(total)
    grad = jnp.concatenate(halves, axis=0) / replicas
    state = state_ref[...] + jnp.mean(grad * grad, axis=1, keepdims=True)
    out_ref[0:mine, :] = (
        previous_ref[...].astype(f32) - learn_rate * grad / (jnp.sqrt(state) + epsilon)
    ).astype(bf16)
    at = iota((chunk, width), 1) == iota((chunk, width), 0) + offset_ref[0]
    sub = iota((16, width), 0)
    lines = jnp.zeros((16, width), f32)
    for core in range(2):
        own = state[core * chunk : (core + 1) * chunk]
        line = jnp.sum(jnp.where(at, own, 0.0), axis=0, keepdims=True)
        first = line.astype(bf16).astype(f32)
        second = (line - first).astype(bf16).astype(f32)
        for k, piece in enumerate((first, second, line - first - second)):
            lines = jnp.where(sub == 3 * core + k, piece, lines)
    out_ref[mine : mine + 16, :] = lines.astype(bf16)


def update_rows(offset, parts, previous, state):
    _, chunk, width = parts.shape
    mine = 2 * chunk
    vmem = pl.BlockSpec(memory_space=pltpu.VMEM)
    return pl.pallas_call(
        update_kernel,
        out_shape=jax.ShapeDtypeStruct((mine + 16, width), bf16),
        in_specs=[pl.BlockSpec(memory_space=pltpu.SMEM), vmem, vmem, vmem],
        compiler_params=params,
        name="update",
    )(offset, parts, previous, state)


def place_kernel(
    mine, starts, every_ref, listed_ref, tiles_ref, table_ref, state_ref, out_ref, state_out, values
):
    step = pl.program_id(0)
    rows, width = table_ref.shape
    touch = listed_ref.shape[1]
    replicas = touch // mine
    stride = mine + 16

    @pl.when(step == 0)
    def _():
        values[touch:, :] = jnp.zeros((256, width), bf16)
        chunk = mine // 2
        for k in range(replicas):
            for core in range(2):
                at = core * (touch // 2) + k * chunk
                source = k * stride + core * chunk
                values[at : at + chunk, :] = every_ref[source : source + chunk, :]
        group = width // chunk
        pieces = []
        for q in range(replicas // group):
            lines = jnp.zeros((16, width), f32)
            for k in range(q * group, (q + 1) * group):
                lines = lines + every_ref[k * stride + mine : (k + 1) * stride, :].astype(f32)
            pieces.append(lines)
        lines = jnp.concatenate(
            [lines[3 * core : 3 * core + 3] for core in range(2) for lines in pieces], axis=1
        )
        high = state_ref.shape[0]
        listed = listed_ref[...]
        at_high = iota((high, touch), 0) == (listed >> 7)
        spread = jnp.concatenate(
            [jnp.where(at_high, lines[k : k + 1, :], 0.0) for k in range(3)], axis=0
        ).astype(bf16)
        at_low = jnp.where(iota((128, touch), 0) == (listed & 127), 1.0, 0.0).astype(bf16)
        placed = dot_nt(spread, at_low)
        state_out[...] = state_ref[...] + (
            placed[0:high] + placed[high : 2 * high] + placed[2 * high : 3 * high]
        )

    for k in range(rows // 128):
        at = step * (rows // 128) + k
        tile = starts[at] >> 7
        row = iota((128, 128), 0) + at * 128
        chosen = jnp.concatenate(
            [
                jnp.where(row == tiles_ref[pl.ds(tile + n, 1), :], 1.0, 0.0).astype(bf16)
                for n in range(2)
            ],
            axis=1,
        )
        window = values[pl.ds(pl.multiple_of(tile * 128, 128), 256), :]
        here = slice(k * 128, (k + 1) * 128)
        out_ref[here, :] = (table_ref[here, :].astype(f32) + dot(chosen, window)).astype(bf16)


def place_rows(starts, every, listed, table, state, mine, tile):
    rows, width = table.shape
    touch = listed.shape[1]
    high = rows // 128
    tiles = jnp.pad(listed.reshape(touch // 128, 128), ((0, 8), (0, 0)), constant_values=-1)
    whole = lambda i, starts: (0, 0)
    return pl.pallas_call(
        functools.partial(place_kernel, mine),
        grid_spec=pltpu.PrefetchScalarGridSpec(
            num_scalar_prefetch=1,
            grid=(rows // tile,),
            in_specs=[
                pl.BlockSpec(every.shape, whole),
                pl.BlockSpec(listed.shape, whole),
                pl.BlockSpec(tiles.shape, whole),
                pl.BlockSpec((tile, width), lambda i, starts: (i, 0)),
                pl.BlockSpec((high, 128), whole),
            ],
            out_specs=(
                pl.BlockSpec((tile, width), lambda i, starts: (i, 0)),
                pl.BlockSpec((high, 128), whole),
            ),
            scratch_shapes=[pltpu.VMEM((touch + 256, width), bf16)],
        ),
        out_shape=(
            jax.ShapeDtypeStruct((rows, width), bf16),
            jax.ShapeDtypeStruct((high, 128), f32),
        ),
        compiler_params=params,
        name="place",
    )(starts, every, listed, tiles, table, state.reshape(high, 128))


def pool_kernel(member_ref, rows_ref, out_ref):
    bag_count = out_ref.shape[0]
    total = dot(member_ref[...], rows_ref[...])
    out_ref[...] = jnp.concatenate([total[0:bag_count], total[64 : 64 + bag_count]], axis=1)


def pool_rows(member, rows, bag_count):
    return pl.pallas_call(
        pool_kernel,
        out_shape=jax.ShapeDtypeStruct((bag_count, 2 * rows.shape[1]), f32),
        compiler_params=params,
        name="pool",
    )(member, rows)


def local(table, row_state, touched_rows, lookup_rows, lookup_bags, route_counts, pooled_grad):
    shards = lax.axis_size("shard")
    replicas = lax.axis_size("replica")
    capacity = lookup_rows.shape[2]
    bag_count, width = pooled_grad.shape
    touch = touched_rows.shape[0]
    mine = touch // replicas
    rows = row_state.shape[0]
    tile = 1024

    bags = jnp.transpose(lookup_bags, (2, 0, 1))
    send = prep(jnp.transpose(lookup_rows, (2, 0, 1)), bags, route_counts, pooled_grad)
    got = lax.all_to_all(send, "shard", split_axis=0, concat_axis=0, tiled=True)

    listed = sort_list(touched_rows)
    replica = lax.axis_index("replica")
    half = touch // 2
    order = listed.reshape(touch)
    core = lax.rem(replica, 2)
    theirs = lax.dynamic_slice(order, ((1 - core) * half,), (half,))
    ours = lax.dynamic_slice(order, (core * half,), (half,))
    turned = jnp.concatenate([theirs, ours])
    column = jnp.broadcast_to(turned.reshape(touch, 1).astype(f32), (touch, 128))
    bounds = jnp.arange(rows // 128, dtype=jnp.int32) * 128
    starts = jnp.sum((touched_rows[None, :] < bounds[:, None]).astype(jnp.int32), axis=1)
    values = jnp.take(table, turned, axis=0, mode="clip")
    chunk = mine // 2
    mine_rows = lax.dynamic_slice(order.reshape(2, half), (0, replica * chunk), (2, chunk))
    mine_rows = mine_rows.reshape(mine)
    mine_values = jnp.concatenate(
        [
            lax.dynamic_slice(values, ((1 - core) * half + replica * chunk, 0), (chunk, width)),
            lax.dynamic_slice(values, (core * half + replica * chunk, 0), (chunk, width)),
        ]
    )
    mine_state = jnp.take(row_state, mine_rows, mode="clip")[:, None]
    marked = jnp.zeros(row_state.shape, f32).at[touched_rows].set(
        1.0, mode="promise_in_bounds", unique_indices=True
    )
    kept_state = jnp.where(marked > 0, 0.0, row_state)
    kept_table = jnp.where(marked[:, None] > 0, jnp.zeros((), bf16), table)
    member = member_matrix(bags, route_counts)
    got, column, values, kept_state, kept_table, mine_state, mine_values, starts, member = (
        lax.optimization_barrier(
            (got, column, values, kept_state, kept_table, mine_state, mine_values, starts, member)
        )
    )

    theirs, ours, picked = sums_and_rows(got, column, values, shards, capacity)
    pairs = [[k, k + 1] for k in range(0, replicas, 2)]
    both = lax.all_gather(theirs, "replica", axis=0, tiled=True, axis_index_groups=pairs)
    theirs = lax.dynamic_slice(both, ((1 - core) * half, 0), (half, width))
    part = (ours + theirs.astype(f32)).astype(bf16)
    parts = lax.all_to_all(
        part.reshape(replicas, chunk, width), "replica", split_axis=0, concat_axis=0, tiled=True
    )
    offset = (lax.rem(replica, width // chunk) * chunk).astype(jnp.int32).reshape(1)
    picked, parts = lax.optimization_barrier((picked, parts))
    returned = lax.all_to_all(picked, "shard", split_axis=0, concat_axis=0, tiled=True)
    updated = update_rows(offset, parts, mine_values, mine_state)
    every = lax.all_gather(updated, "replica", axis=0, tiled=True)
    new_table, new_state = place_rows(starts, every, listed, kept_table, kept_state, mine, tile)
    pooled = pool_rows(member, returned.reshape(-1, width // 2), bag_count)
    return (pooled, new_table, new_state.reshape(row_state.shape))


def solution(mesh):
    return jax.shard_map(
        local,
        mesh=mesh,
        in_specs=(
            P("shard", None),
            P("shard"),
            P("shard"),
            P("replica", "shard", None),
            P("replica", "shard", None),
            P("replica", "shard"),
            P(("replica", "shard"), None),
        ),
        out_specs=(P(("replica", "shard"), None), P("shard", None), P("shard")),
        check_vma=False,
    )
```

```python
import functools

import jax
import jax.numpy as jnp
from jax import lax
from jax.experimental import pallas as pl
from jax.experimental.pallas import tpu as pltpu
from jax.sharding import PartitionSpec as P

learn_rate = 0.5
epsilon = 1e-08
bf16 = jnp.bfloat16
f32 = jnp.float32

block = 24
dead = 200
large = pltpu.CompilerParams(vmem_limit_bytes=60 * 1024 * 1024)
params = pltpu.CompilerParams(vmem_limit_bytes=24 * 1024 * 1024)


def iota(shape, axis):
    return lax.broadcasted_iota(jnp.int32, shape, axis)


def dot(a, b):
    return jnp.dot(a, b, preferred_element_type=f32)


def pair_of(position):
    return (position * 2731) >> 16


def keys_of(bags_ref, counts_ref):
    capacity, _, shards = bags_ref.shape
    bags = bags_ref[...].reshape(capacity, shards)
    live = iota((capacity, shards), 0) < counts_ref[...]
    return jnp.where(live, bags, dead).astype(f32).astype(bf16)


def dot_nt(a, b):
    return lax.dot_general(a, b, (((1,), (1,)), ((), ())), preferred_element_type=f32)


def dot_tn(a, b):
    return lax.dot_general(a, b, (((0,), (0,)), ((), ())), preferred_element_type=f32)


def prep_kernel(rows_ref, bags_ref, counts_ref, grad_ref, out_ref, held, sems):
    capacity, _, shards = rows_ref.shape
    bag_count, width = grad_ref.shape
    flat = shards * block
    groups = held.shape[1]
    key = keys_of(bags_ref, counts_ref)
    position, lane = iota((flat, 128), 0), iota((flat, 128), 1)
    pair = pair_of(position)
    slot = position - block * pair
    spread = jnp.where(pair == lane, 1.0, 0.0)
    per_row = dot_nt(spread.astype(bf16)[:, 0:shards], key)
    per_row = jnp.where((slot == lane)[:, 0:capacity], per_row, 0.0).astype(bf16)
    bag = dot(per_row, jnp.ones((capacity, 128), bf16))
    bag = jnp.where(slot < capacity, bag, float(dead))
    member = jnp.where(bag == lane.astype(f32), 1.0, 0.0).astype(bf16)
    grads = jnp.concatenate(
        [grad_ref[...], jnp.zeros((128 - bag_count, width), f32)], axis=0
    ).astype(bf16)
    rows = rows_ref[...].reshape(capacity, shards)
    high = (rows >> 6).astype(f32).astype(bf16)
    low = (rows & 63).astype(f32).astype(bf16)
    lane = iota((width, capacity), 0)
    sub = iota((width, capacity), 1)
    meta = dot(jnp.where(lane == sub, 1.0, 0.0).astype(bf16), high) + dot(
        jnp.where(lane == sub + 64, 1.0, 0.0).astype(bf16), low
    )
    at_meta = jnp.where(slot == capacity, spread, 0.0).astype(bf16)[:, 0:shards]
    meta = meta.astype(bf16)
    pieces = sems.shape[0]
    size = flat // pieces
    copies = []
    for k in range(pieces):
        here = slice(k * size, (k + 1) * size)
        rows = dot(member[here], grads) + dot_nt(at_meta[here], meta)
        pairs = shards // pieces
        rows = rows.reshape(pairs, block, width)
        to = slice(k * pairs, (k + 1) * pairs)
        for g in range(groups - 1):
            q, h = g // 2, (g % 2) * 128
            held[to, g] = rows[:, 2 * q : 2 * q + 2, h : h + 128].astype(bf16)
        held[to, groups - 1] = rows[:, capacity : capacity + 2, 0:128].astype(bf16)
        at = pl.ds(k * pairs, pairs)
        copies.append(pltpu.make_async_copy(held.at[at], out_ref.at[at], sems.at[k]))
        copies[-1].start()
    for copy in copies:
        copy.wait()


def prep(rows, bags, counts, grad):
    capacity, _, shards = rows.shape
    shape = (shards, capacity + 1, 2, 128)
    return pl.pallas_call(
        prep_kernel,
        out_shape=jax.ShapeDtypeStruct(shape, bf16),
        out_specs=pl.BlockSpec(memory_space=pltpu.HBM),
        scratch_shapes=[pltpu.VMEM(shape, bf16), pltpu.SemaphoreType.DMA((4,))],
        compiler_params=large,
        name="prep",
    )(rows, bags, counts, grad)


def packed_slot(position, capacity):
    whole = 16
    rest = capacity - whole
    tail = position - 2 * whole
    right = ((position >= whole) & (position < 2 * whole)) | (tail >= rest)
    slot = jnp.where(
        position < 2 * whole,
        position & (whole - 1),
        whole + jnp.where(tail >= rest, tail - rest, tail),
    )
    return slot, right


def member_kernel(bags_ref, counts_ref, out_ref):
    capacity, _, shards = bags_ref.shape
    pack = 2 * capacity
    flat = shards * pack
    key = keys_of(bags_ref, counts_ref)

    def pair_and_place(shape, axis):
        row = iota(shape, axis)
        pair = (row * 13108) >> 19
        return pair, row - pack * pair

    shape = (shards, flat)
    spread = jnp.where(pair_and_place(shape, 1)[0] == iota(shape, 0), 1.0, 0.0).astype(bf16)
    per_row = dot(key, spread)
    shape = (capacity, flat)
    slot, _ = packed_slot(pair_and_place(shape, 1)[1], capacity)
    own = jnp.where(slot == iota(shape, 0), per_row, 0.0).astype(bf16)
    bag = dot(jnp.ones((128, capacity), bf16), own)
    shape = (128, flat)
    _, right = packed_slot(pair_and_place(shape, 1)[1], capacity)
    bag = bag + jnp.where(right, 64.0, 0.0)
    out_ref[...] = jnp.where(bag == iota(shape, 0).astype(f32), 1.0, 0.0).astype(bf16)


def member_matrix(bags, counts):
    capacity, _, shards = bags.shape
    return pl.pallas_call(
        member_kernel,
        out_shape=jax.ShapeDtypeStruct((128, shards * 2 * capacity), bf16),
        compiler_params=params,
        name="member",
    )(bags, counts)


def sort_kernel(line_ref, column_ref, line_out):
    touch = line_ref.shape[1]
    tiles = touch // 128
    column = jnp.broadcast_to(column_ref[...], (touch, 128))
    lanes = iota((touch, 128), 1).astype(f32)
    below = jnp.zeros((touch, 128), f32)
    for k in range(tiles):
        line = line_ref[:, k * 128 : (k + 1) * 128]
        below = below + jnp.where(line < column, 1.0, 0.0)
    rank_column = jnp.sum(below, axis=1, keepdims=True)
    for k in range(tiles):
        at = rank_column == lanes + 128.0 * k
        line_out[:, k * 128 : (k + 1) * 128] = jnp.sum(
            jnp.where(at, column, 0.0), axis=0, keepdims=True
        ).astype(jnp.int32)


def sort_list(touched):
    touch = touched.shape[0]
    values = touched.astype(f32)
    return pl.pallas_call(
        sort_kernel,
        out_shape=jax.ShapeDtypeStruct((1, touch), jnp.int32),
        compiler_params=params,
        name="sort",
    )(values.reshape(1, touch), values.reshape(touch, 1))


def hit_matrix(got_ref, column_ref, hits, capacity):
    shards, groups, _, half = got_ref.shape
    flat = shards * block
    left = [got_ref[:, g].astype(f32) for g in range(0, groups - 1, 2)]
    right = [got_ref[:, g].astype(f32) for g in range(1, groups - 1, 2)]
    meta = got_ref[:, groups - 1].astype(f32)
    none = jnp.zeros((shards, block - capacity, half), f32)
    got = jnp.concatenate(
        [jnp.concatenate(left + [none], axis=1), jnp.concatenate(right + [none], axis=1)], axis=2
    )
    got = got.reshape(flat, 2 * half).astype(bf16)
    column = column_ref[...]
    shape = (shards, block, half)
    own = (iota(shape, 2) & 63) == iota(shape, 1)
    spread = jnp.where(own, jnp.broadcast_to(meta[:, 0:1, :], shape), 0.0)
    spread = spread.reshape(flat, half).astype(bf16)
    weigh = jnp.where(iota((8, half), 1) < 64, 64.0, 1.0).astype(bf16)
    rows = dot_nt(weigh, spread)
    lane = iota((8, flat), 1)
    rows = jnp.where(lane - block * pair_of(lane) < capacity, rows, -1.0)
    for k in range(flat // 128):
        line = rows[0:1, k * 128 : (k + 1) * 128]
        hits[:, k * 128 : (k + 1) * 128] = jnp.where(column == line, 1.0, 0.0).astype(bf16)
    return got


def hits_kernel(
    capacity, got_ref, column_ref, values_ref, theirs_ref, ours_ref, picked_ref, hits
):
    got = hit_matrix(got_ref, column_ref, hits, capacity)
    half = theirs_ref.shape[0]
    theirs_ref[...] = dot(hits[0:half, :], got).astype(bf16)
    ours_ref[...] = dot(hits[half:, :], got)
    shards, pack, width = picked_ref.shape
    whole = 16
    rest = pack // 2 - whole
    rows = dot_tn(hits[...], values_ref[...]).reshape(shards, block, 2 * width)
    left, right = rows[:, :, 0:width], rows[:, :, width : 2 * width]
    first = iota((shards, block - whole, width), 1) < rest
    mixed = jnp.where(
        first, left[:, whole:block, :], pltpu.roll(right[:, whole:block, :], rest, 1)
    )
    picked_ref[...] = jnp.concatenate(
        [left[:, 0:whole, :], right[:, 0:whole, :], mixed], axis=1
    ).astype(bf16)


def sums_and_rows(got, column, values, shards, capacity):
    flat, width = shards * block, values.shape[1]
    touch = column.shape[0]
    return pl.pallas_call(
        functools.partial(hits_kernel, capacity),
        out_shape=(
            jax.ShapeDtypeStruct((touch // 2, width), bf16),
            jax.ShapeDtypeStruct((touch // 2, width), f32),
            jax.ShapeDtypeStruct((shards, 2 * capacity, width // 2), bf16),
        ),
        scratch_shapes=[pltpu.VMEM((touch, flat), bf16)],
        compiler_params=params,
        name="hits",
    )(got, column, values)


def update_kernel(offset_ref, parts_ref, previous_ref, state_ref, out_ref):
    replicas, chunk, width = parts_ref.shape
    mine = 2 * chunk
    halves = []
    for core in range(2):
        total = parts_ref[core].astype(f32)
        for k in range(core + 2, replicas, 2):
            total = total + parts_ref[k].astype(f32)
        halves.append(total)
    grad = jnp.concatenate(halves, axis=0) / replicas
    state = state_ref[...] + jnp.mean(grad * grad, axis=1, keepdims=True)
    out_ref[0:mine, :] = (
        previous_ref[...].astype(f32) - learn_rate * grad / (jnp.sqrt(state) + epsilon)
    ).astype(bf16)
    at = iota((chunk, width), 1) == iota((chunk, width), 0) + offset_ref[0]
    sub = iota((16, width), 0)
    lines = jnp.zeros((16, width), f32)
    for core in range(2):
        own = state[core * chunk : (core + 1) * chunk]
        line = jnp.sum(jnp.where(at, own, 0.0), axis=0, keepdims=True)
        first = line.astype(bf16).astype(f32)
        second = (line - first).astype(bf16).astype(f32)
        for k, piece in enumerate((first, second, line - first - second)):
            lines = jnp.where(sub == 3 * core + k, piece, lines)
    out_ref[mine : mine + 16, :] = lines.astype(bf16)


def update_rows(offset, parts, previous, state):
    _, chunk, width = parts.shape
    mine = 2 * chunk
    vmem = pl.BlockSpec(memory_space=pltpu.VMEM)
    return pl.pallas_call(
        update_kernel,
        out_shape=jax.ShapeDtypeStruct((mine + 16, width), bf16),
        in_specs=[pl.BlockSpec(memory_space=pltpu.SMEM), vmem, vmem, vmem],
        compiler_params=params,
        name="update",
    )(offset, parts, previous, state)


def place_kernel(
    mine, starts, every_ref, listed_ref, tiles_ref, table_ref, state_ref, out_ref, state_out, values
):
    step = pl.program_id(0)
    rows, width = table_ref.shape
    touch = listed_ref.shape[1]
    replicas = touch // mine
    stride = mine + 16

    @pl.when(step == 0)
    def _():
        values[touch:, :] = jnp.zeros((256, width), bf16)
        chunk = mine // 2
        for k in range(replicas):
            for core in range(2):
                at = core * (touch // 2) + k * chunk
                source = k * stride + core * chunk
                values[at : at + chunk, :] = every_ref[source : source + chunk, :]
        group = width // chunk
        pieces = []
        for q in range(replicas // group):
            lines = jnp.zeros((16, width), f32)
            for k in range(q * group, (q + 1) * group):
                lines = lines + every_ref[k * stride + mine : (k + 1) * stride, :].astype(f32)
            pieces.append(lines)
        lines = jnp.concatenate(
            [lines[3 * core : 3 * core + 3] for core in range(2) for lines in pieces], axis=1
        )
        high = state_ref.shape[0]
        listed = listed_ref[...]
        at_high = iota((high, touch), 0) == (listed >> 7)
        spread = jnp.concatenate(
            [jnp.where(at_high, lines[k : k + 1, :], 0.0) for k in range(3)], axis=0
        ).astype(bf16)
        at_low = jnp.where(iota((128, touch), 0) == (listed & 127), 1.0, 0.0).astype(bf16)
        placed = dot_nt(spread, at_low)
        state_out[...] = state_ref[...] + (
            placed[0:high] + placed[high : 2 * high] + placed[2 * high : 3 * high]
        )

    for k in range(rows // 128):
        at = step * (rows // 128) + k
        tile = starts[at] >> 7
        row = iota((128, 128), 0) + at * 128
        chosen = jnp.concatenate(
            [
                jnp.where(row == tiles_ref[pl.ds(tile + n, 1), :], 1.0, 0.0).astype(bf16)
                for n in range(2)
            ],
            axis=1,
        )
        window = values[pl.ds(pl.multiple_of(tile * 128, 128), 256), :]
        here = slice(k * 128, (k + 1) * 128)
        out_ref[here, :] = (table_ref[here, :].astype(f32) + dot(chosen, window)).astype(bf16)


def place_rows(starts, every, listed, table, state, mine, tile):
    rows, width = table.shape
    touch = listed.shape[1]
    high = rows // 128
    tiles = jnp.pad(listed.reshape(touch // 128, 128), ((0, 8), (0, 0)), constant_values=-1)
    whole = lambda i, starts: (0, 0)
    return pl.pallas_call(
        functools.partial(place_kernel, mine),
        grid_spec=pltpu.PrefetchScalarGridSpec(
            num_scalar_prefetch=1,
            grid=(rows // tile,),
            in_specs=[
                pl.BlockSpec(every.shape, whole),
                pl.BlockSpec(listed.shape, whole),
                pl.BlockSpec(tiles.shape, whole),
                pl.BlockSpec((tile, width), lambda i, starts: (i, 0)),
                pl.BlockSpec((high, 128), whole),
            ],
            out_specs=(
                pl.BlockSpec((tile, width), lambda i, starts: (i, 0)),
                pl.BlockSpec((high, 128), whole),
            ),
            scratch_shapes=[pltpu.VMEM((touch + 256, width), bf16)],
        ),
        out_shape=(
            jax.ShapeDtypeStruct((rows, width), bf16),
            jax.ShapeDtypeStruct((high, 128), f32),
        ),
        compiler_params=params,
        name="place",
    )(starts, every, listed, tiles, table, state.reshape(high, 128))


def pool_kernel(member_ref, rows_ref, out_ref):
    bag_count = out_ref.shape[0]
    total = dot(member_ref[...], rows_ref[...])
    out_ref[...] = jnp.concatenate([total[0:bag_count], total[64 : 64 + bag_count]], axis=1)


def pool_rows(member, rows, bag_count):
    return pl.pallas_call(
        pool_kernel,
        out_shape=jax.ShapeDtypeStruct((bag_count, 2 * rows.shape[1]), f32),
        compiler_params=params,
        name="pool",
    )(member, rows)


def local(table, row_state, touched_rows, lookup_rows, lookup_bags, route_counts, pooled_grad):
    shards = lax.axis_size("shard")
    replicas = lax.axis_size("replica")
    capacity = lookup_rows.shape[2]
    bag_count, width = pooled_grad.shape
    touch = touched_rows.shape[0]
    mine = touch // replicas
    rows = row_state.shape[0]
    tile = 1024

    bags = jnp.transpose(lookup_bags, (2, 0, 1))
    send = prep(jnp.transpose(lookup_rows, (2, 0, 1)), bags, route_counts, pooled_grad)
    got = lax.all_to_all(send, "shard", split_axis=0, concat_axis=0, tiled=True)

    listed = sort_list(touched_rows)
    replica = lax.axis_index("replica")
    half = touch // 2
    order = listed.reshape(touch)
    core = lax.rem(replica, 2)
    theirs = lax.dynamic_slice(order, ((1 - core) * half,), (half,))
    ours = lax.dynamic_slice(order, (core * half,), (half,))
    turned = jnp.concatenate([theirs, ours])
    column = jnp.broadcast_to(turned.reshape(touch, 1).astype(f32), (touch, 128))
    bounds = jnp.arange(rows // 128, dtype=jnp.int32) * 128
    starts = jnp.sum((touched_rows[None, :] < bounds[:, None]).astype(jnp.int32), axis=1)
    values = jnp.take(table, turned, axis=0, mode="clip")
    chunk = mine // 2
    mine_rows = lax.dynamic_slice(order.reshape(2, half), (0, replica * chunk), (2, chunk))
    mine_rows = mine_rows.reshape(mine)
    mine_values = jnp.concatenate(
        [
            lax.dynamic_slice(values, ((1 - core) * half + replica * chunk, 0), (chunk, width)),
            lax.dynamic_slice(values, (core * half + replica * chunk, 0), (chunk, width)),
        ]
    )
    mine_state = jnp.take(row_state, mine_rows, mode="clip")[:, None]
    marked = jnp.zeros(row_state.shape, f32).at[touched_rows].set(
        1.0, mode="promise_in_bounds", unique_indices=True
    )
    kept_state = jnp.where(marked > 0, 0.0, row_state)
    kept_table = jnp.where(marked[:, None] > 0, jnp.zeros((), bf16), table)
    member = member_matrix(bags, route_counts)
    got, column, values, kept_state, kept_table, mine_state, mine_values, starts, member = (
        lax.optimization_barrier(
            (got, column, values, kept_state, kept_table, mine_state, mine_values, starts, member)
        )
    )

    theirs, ours, picked = sums_and_rows(got, column, values, shards, capacity)
    pairs = [[k, k + 1] for k in range(0, replicas, 2)]
    both = lax.all_gather(theirs, "replica", axis=0, tiled=True, axis_index_groups=pairs)
    theirs = lax.dynamic_slice(both, ((1 - core) * half, 0), (half, width))
    part = (ours + theirs.astype(f32)).astype(bf16)
    parts = lax.all_to_all(
        part.reshape(replicas, chunk, width), "replica", split_axis=0, concat_axis=0, tiled=True
    )
    offset = (lax.rem(replica, width // chunk) * chunk).astype(jnp.int32).reshape(1)
    picked, parts = lax.optimization_barrier((picked, parts))
    returned = lax.all_to_all(picked, "shard", split_axis=0, concat_axis=0, tiled=True)
    updated = update_rows(offset, parts, mine_values, mine_state)
    every = lax.all_gather(updated, "replica", axis=0, tiled=True)
    new_table, new_state = place_rows(starts, every, listed, kept_table, kept_state, mine, tile)
    pooled = pool_rows(member, returned.reshape(-1, width // 2), bag_count)
    return (pooled, new_table, new_state.reshape(row_state.shape))


def solution(mesh):
    return jax.shard_map(
        local,
        mesh=mesh,
        in_specs=(
            P("shard", None),
            P("shard"),
            P("shard"),
            P("replica", "shard", None),
            P("replica", "shard", None),
            P("replica", "shard"),
            P(("replica", "shard"), None),
        ),
        out_specs=(P(("replica", "shard"), None), P("shard", None), P("shard")),
        check_vma=False,
    )
```
